256 devices in a mesh: env: 2 (over x_lo), row: 8 (over y, core), col: 16 (over z, x_hi).
Axes of the slice: x: 4 (x_hi: 2, x_lo: 2; x = x_hi * 2 + x_lo), y: 4, z: 8, core: 2. Of those that a mesh axis runs over, the one named last changes fastest.
Arguments:
- adjoint_hat: float32 [2, 3, 2, 256, 256, 256], P('env', None, None, 'row', 'col'), may hold values from -6 to 6
- velocity: float32 [2, 3, 256, 256, 256], P('env', None, 'row', 'col'), may hold values from -6 to 6
- vorticity: float32 [2, 3, 256, 256, 256], P('env', None, 'row', 'col'), may hold values from -6 to 6
Outputs:
- adjoint_out: float32 [2, 3, 2, 256, 256, 256], P('env', None, None, 'row', 'col')
- controller_grad: float32 [3, 6], replicated
The draws below stay inside these ranges and needn't reach their ends.
All inputs are finite; a program needn't handle non-finite values.
Results may differ from the reference program's by a relative error of at most 0.00027.
Values sent between devices are 32-bit elements; how exact they have to be, the bound alone decides.
A program may use at most 128 MiB of HBM per device.

```python
import math
import jax
import jax.numpy as jnp
from jax import lax

N = 256
ENVS = 2


def levels(stream_key, extent, cuts, smallest, high):
    loudness = 1.0
    for dim, shards_of in cuts:
        heights = jax.random.uniform(jax.random.fold_in(jax.random.fold_in(stream_key, 6), dim), (shards_of,), jnp.float32, smallest / len(cuts), high / len(cuts))
        loudness = loudness * jnp.repeat(jnp.exp(heights), extent[dim] // shards_of).reshape((-1,) + (1,) * (len(extent) - 1 - dim))
    return loudness


def gaussian(rng, shape, scale, most, shards=(), kind=jnp.bfloat16):
    entries = scale * jax.random.normal(rng, shape, jnp.float32)
    if shards:
        entries = entries * levels(rng, shape, shards, -0.22, 0.18)
    return jnp.clip(entries, -most, most).astype(kind)


def setup_inputs(seed: int = 0) -> dict:
    key_of = jax.random.split(jax.random.key(seed), 4)
    return {
        "adjoint_hat": gaussian(key_of[0], (ENVS, 3, 2, N, N, N), 1.0, 6.0, ((0, 2), (3, 8), (4, 16)), jnp.float32),
        "velocity": gaussian(key_of[1], (ENVS, 3, N, N, N), 1.0, 6.0, ((0, 2), (2, 8), (3, 16)), jnp.float32),
        "vorticity": gaussian(key_of[2], (ENVS, 3, N, N, N), 1.0, 6.0, ((0, 2), (2, 8), (3, 16)), jnp.float32),
    }


def wavenumber(length):
    indices = jnp.arange(length, dtype=jnp.int32)
    return jnp.where(indices < length // 2, indices, indices - length).astype(jnp.float32)

def reference(adjoint_hat, velocity, vorticity):
    env_count = adjoint_hat.shape[0]
    length = adjoint_hat.shape[-1]
    numbers = wavenumber(length)
    wave_y = numbers[:, None, None]
    wave_z = numbers[None, :, None]
    wave_x = numbers[None, None, :]
    kept_mask = ((3.0 * jnp.abs(wave_x) < length) & (3.0 * jnp.abs(wave_y) < length) & (3.0 * jnp.abs(wave_z) < length)).astype(jnp.float32)
    wave_square = jnp.maximum(wave_x * wave_x + wave_y * wave_y + wave_z * wave_z, 1.0)
    waves = (wave_x, wave_y, wave_z)
    norm_factor = 1.0 / math.sqrt(env_count * length ** 3)
    controller_grad = jnp.zeros((3, 6), jnp.float32)
    results = []
    for member in range(env_count):
        fields = []
        for component in range(3):
            spectrum = adjoint_hat[member, component, 0] + 1j * adjoint_hat[member, component, 1]
            physical = jnp.fft.ifftn(spectrum, norm='ortho').real
            fields.append(jnp.transpose(physical, (2, 0, 1)).astype(jnp.float32))
        adjoint = jnp.stack(fields)
        features = jnp.concatenate((velocity[member], vorticity[member]), 0)
        controller_grad = controller_grad + jnp.einsum('cabz,jabz->cj', adjoint, features, precision=lax.Precision.HIGHEST) * norm_factor
        adj_x, adj_y, adj_z = fields
        spin_x, spin_y, spin_z = (vorticity[member, 0], vorticity[member, 1], vorticity[member, 2])
        crossed = (spin_y * adj_z - spin_z * adj_y, spin_z * adj_x - spin_x * adj_z, spin_x * adj_y - spin_y * adj_x)
        spectra = [jnp.fft.fftn(jnp.transpose(piece, (1, 2, 0)), norm='ortho') for piece in crossed]
        inner = wave_x * spectra[0] + wave_y * spectra[1] + wave_z * spectra[2]
        projected = [(spectra[component] - waves[component] * inner / wave_square) * kept_mask for component in range(3)]
        results.append(jnp.stack([jnp.stack((piece.real, piece.imag)) for piece in projected]).astype(jnp.float32))
    return (jnp.stack(results), controller_grad)
```

```python
import math

import jax
import jax.numpy as jnp
import ml_dtypes
import numpy as np
from jax import lax
from jax.experimental import pallas as pl
from jax.experimental.pallas import tpu as pltpu
from jax.sharding import PartitionSpec as P

F32 = jnp.float32
BF16 = jnp.bfloat16
MESH = pl.DeviceIdType.MESH

N = 256
ROWS = 8
COLS = 16
KYS = 32
KZS = 16
PARTS = 4
ACTIVE_COLS = (0, 1, 2, 3, 4, 5, 10, 11, 12, 13, 14, 15)
ACTIVE_ROWS = (0, 1, 2, 5, 6, 7)
NCOL = len(ACTIVE_COLS)
NROW = len(ACTIVE_ROWS)


def halves(table):
    high = table.astype(np.float32).astype(ml_dtypes.bfloat16)
    low = (table - high.astype(np.float64)).astype(np.float32).astype(ml_dtypes.bfloat16)
    return high, low


def stacked(table, axis):
    high, low = halves(table)
    return np.concatenate((high, low, high), axis)


def wave(out_index, in_index):
    angles = (np.outer(out_index, in_index) % N) * (2.0 * math.pi / N)
    return np.cos(angles) / math.sqrt(N), np.sin(angles) / math.sqrt(N)


def x_order():
    order = np.zeros((2, 8, 16), np.int64)
    for half in range(2):
        for inner in range(8):
            for slot in range(16):
                order[half, inner, slot] = 32 * (slot & 7) + 8 * (2 * half + (slot >> 3)) + inner
    return order.reshape(2, 128)


def tables():
    every = np.arange(N)
    order = x_order()
    table_a = []
    for half in range(2):
        cosines, sines = wave(every, order[half])
        block = np.block([[cosines, sines], [-sines, cosines]])
        table_a.append(stacked(block, 0))
    table_a = np.stack(table_a)
    cosines, sines = wave(every, every)
    table_b = stacked(np.block([[cosines, -sines], [sines, cosines]]), 1)
    table_c = stacked(np.concatenate((cosines, -sines), 0), 0)
    pieces = []
    for col in ACTIVE_COLS:
        kept = slice(KZS * col, KZS * col + KZS)
        pieces += [cosines[:, kept], -sines[:, kept]]
    table_z = stacked(np.concatenate(pieces, 1), 0)
    pieces = []
    for row in ACTIVE_ROWS:
        kept = slice(KYS * row, KYS * row + KYS)
        pieces.append(np.concatenate((cosines[kept], sines[kept]), 1))
        pieces.append(np.concatenate((-sines[kept], cosines[kept]), 1))
    table_d = stacked(np.concatenate(pieces, 0), 1)
    cosines, sines = wave(order.reshape(-1), every)
    table_e = stacked(np.block([[cosines, -sines], [sines, cosines]]), 0)
    return table_a, table_b, table_c, table_z, table_d, table_e


def exchange(values, lane_bits):
    values = list(values)
    lane = lax.broadcasted_iota(jnp.int32, values[0].shape, 1)
    bit = 1
    while bit < len(values):
        step = bit * lane_bits
        clear = (lane & step) == 0
        for low in range(len(values)):
            if low & bit:
                continue
            first, second = values[low], values[low | bit]
            values[low] = jnp.where(clear, first, pltpu.roll(second, step, 1))
            values[low | bit] = jnp.where(clear, pltpu.roll(first, 128 - step, 1), second)
        bit *= 2
    return values


def split(value):
    high = value.astype(BF16)
    low = (value - high.astype(F32)).astype(BF16)
    return high, low


def matmul(left, right):
    return jnp.dot(left, right, preferred_element_type=F32)


def active_col(slot):
    return jnp.where(slot < 6, slot, slot + 4)


def active_row(slot):
    return jnp.where(slot < 3, slot, slot + 2)


def body(
    g_hbm, vel_hbm, vort_hbm, ta_hbm, tb_hbm, tc_hbm, tz_hbm, td_hbm,
    arrived, grad_out,
    g, feat, ta, tb, tc, tz, td,
    lhs_a, work_a, send_a, recv_a, rhs, send_b, recv_b,
    lhs_c, work_c, lhs_z, work_z, send_c, recv_c, send_d,
    grad_acc, grad_part, grad_row, grad_sum_row, grad_col, grad_sum_col, grad_env,
    load_sem, ra_sem, rb_sem, rc_sem, rd_sem, sa_sem, sb_sem, sc_sem, sd_sem,
    grad_recv, grad_send,
):
    env = lax.axis_index("env")
    row = lax.axis_index("row")
    col = lax.axis_index("col")
    col_active = (col < 6) | (col >= 10)
    row_active = (row < 3) | (row >= 5)

    loads = [pltpu.make_async_copy(ta_hbm, ta, load_sem.at[0])]
    for c in range(3):
        loads.append(pltpu.make_async_copy(g_hbm.at[c], g.at[c], load_sem.at[1 + c]))
    loads.append(pltpu.make_async_copy(tb_hbm, tb, load_sem.at[4]))
    loads.append(pltpu.make_async_copy(tc_hbm, tc, load_sem.at[5]))
    loads.append(pltpu.make_async_copy(vel_hbm, feat.at[pl.ds(0, 3)], load_sem.at[6]))
    loads.append(pltpu.make_async_copy(vort_hbm, feat.at[pl.ds(3, 3)], load_sem.at[7]))
    loads.append(pltpu.make_async_copy(tz_hbm, tz, load_sem.at[8]))
    loads.append(pltpu.make_async_copy(td_hbm, td, load_sem.at[9]))
    for load in loads:
        load.start()

    barrier = pltpu.get_barrier_semaphore()

    def greet_row(k, _):
        pl.semaphore_signal(
            barrier, inc=1, device_id={"row": lax.rem(row + k, ROWS)}, device_id_type=MESH
        )
        return 0

    def greet_col(k, _):
        pl.semaphore_signal(
            barrier, inc=1, device_id={"col": lax.rem(col + k, COLS)}, device_id_type=MESH
        )
        return 0

    lax.fori_loop(1, ROWS, greet_row, 0)
    lax.fori_loop(1, COLS, greet_col, 0)
    pl.semaphore_signal(barrier, inc=1, device_id={"env": 1 - env}, device_id_type=MESH)

    def spectrum_x(half, c):
        out = matmul(lhs_a[c], ta[half])
        work_a[0] = out[:, :128]
        work_a[1] = out[:, 128:]

        def pack(step, _):
            t = step // 4
            tile = step % 4
            values = [
                work_a[t, pl.ds(tile * 128 + kz, 8, stride=16), :] for kz in range(16)
            ]
            values = exchange(values, 1)
            for slot in range(16):
                send_a[2 * half + (slot >> 3), slot & 7, c, t, pl.ds(tile * 8, 8), :] = values[slot]
            return 0

        lax.fori_loop(0, 8, pack, 0)

    def start_row(j):
        def one(k, _):
            to = lax.rem(row + k, ROWS)
            pltpu.make_async_remote_copy(
                src_ref=send_a.at[j, to],
                dst_ref=recv_a.at[j, :, :, pl.ds(KYS * row, KYS), :],
                send_sem=sa_sem,
                recv_sem=ra_sem.at[j],
                device_id={"row": to},
                device_id_type=MESH,
            ).start()
            return 0

        lax.fori_loop(1, ROWS, one, 0)
        pltpu.make_async_copy(
            send_a.at[j, row], recv_a.at[j, :, :, pl.ds(KYS * row, KYS), :], ra_sem.at[j]
        ).start()

    loads[0].wait()
    for half in range(2):
        for c in range(3):
            if half == 0:
                loads[1 + c].wait()
                for s in range(2):
                    high, low = split(g[c, s])
                    lhs_a[c, :, 256 * s : 256 * s + 256] = high
                    lhs_a[c, :, 512 + 256 * s : 768 + 256 * s] = high
                    lhs_a[c, :, 1024 + 256 * s : 1280 + 256 * s] = low
            spectrum_x(half, c)
        if half == 0:
            pl.semaphore_wait(barrier, ROWS - 1 + COLS - 1 + 1)
        start_row(2 * half)
        start_row(2 * half + 1)

    loads[4].wait()

    def stage_b(j, _):
        pltpu.make_async_copy(recv_a.at[j], recv_a.at[j], ra_sem.at[j]).wait()
        for c in range(3):
            for s in range(2):
                high, low = split(recv_a[j, c, s])
                rhs[256 * s : 256 * s + 256, 128 * c : 128 * c + 128] = high
                rhs[512 + 256 * s : 768 + 256 * s, 128 * c : 128 * c + 128] = high
                rhs[1024 + 256 * s : 1280 + 256 * s, 128 * c : 128 * c + 128] = low
        out = matmul(tb[...], rhs[...])
        for c in range(3):
            for t in range(2):
                send_b[j, c, t] = out[256 * t : 256 * t + 256, 128 * c : 128 * c + 128]

        def one(k, _):
            to = lax.rem(col + k, COLS)
            pltpu.make_async_remote_copy(
                src_ref=send_b.at[j, :, :, pl.ds(KZS * to, KZS), :],
                dst_ref=recv_b.at[j, col],
                send_sem=sb_sem,
                recv_sem=rb_sem.at[j],
                device_id={"col": to},
                device_id_type=MESH,
            ).start()
            return 0

        lax.fori_loop(1, COLS, one, 0)
        pltpu.make_async_copy(
            send_b.at[j, :, :, pl.ds(KZS * col, KZS), :], recv_b.at[j, col], rb_sem.at[j]
        ).start()
        return 0

    lax.fori_loop(0, PARTS, stage_b, 0)

    for load in loads[5:9]:
        load.wait()
    grad_acc[...] = jnp.zeros_like(grad_acc)

    def stage_c(j, _):
        pltpu.make_async_copy(recv_b.at[j], recv_b.at[j], rb_sem.at[j]).wait()

        def gather(step, _):
            c = step // 2
            s = step % 2
            for group in range(2):
                values = [recv_b[j, 8 * group + k, c, s] for k in range(8)]
                values = exchange(values, 16)
                for x in range(8):
                    high, low = split(values[x])
                    rows = pl.ds(pl.multiple_of(128 * c + 16 * x, 16), 16)
                    at = pl.multiple_of(256 * s + 128 * group, 128)
                    lhs_c[rows, pl.ds(at, 128)] = high
                    lhs_c[rows, pl.ds(at + 512, 128)] = high
                    lhs_c[rows, pl.ds(at + 1024, 128)] = low
            return 0

        lax.fori_loop(0, 6, gather, 0)
        work_c[...] = matmul(lhs_c[...], tc[...])

        def cross(i, _):
            here = pl.ds(pl.multiple_of(16 * i, 16), 16)
            there = pl.ds(pl.multiple_of(128 * j + 16 * i, 16), 16)
            adjoint = [work_c[pl.ds(pl.multiple_of(128 * c + 16 * i, 16), 16), :] for c in range(3)]
            for f in range(6):
                feature = feat[f, there, :]
                for c in range(3):
                    product = adjoint[c] * feature
                    total = (product[:8, :128] + product[:8, 128:]) + (
                        product[8:, :128] + product[8:, 128:]
                    )
                    grad_acc[6 * c + f] += total
            spin = [feat[3 + c, there, :] for c in range(3)]
            for c in range(3):
                second, third = (c + 1) % 3, (c + 2) % 3
                high, low = split(
                    spin[second] * adjoint[third] - spin[third] * adjoint[second]
                )
                rows = pl.ds(pl.multiple_of(128 * c + 16 * i, 16), 16)
                lhs_z[rows, 0:256] = high
                lhs_z[rows, 256:512] = high
                lhs_z[rows, 512:768] = low
            return 0

        lax.fori_loop(0, 8, cross, 0)
        work_z[...] = matmul(lhs_z[...], tz[...])

        def scatter(c, _):
            for n in range(3):
                values = [
                    work_z[
                        pl.ds(pl.multiple_of(128 * c + 16 * x, 16), 16), 128 * n : 128 * n + 128
                    ]
                    for x in range(8)
                ]
                values = exchange(values, 16)
                for b in range(8):
                    block = 8 * n + b
                    send_c[j, block >> 1, block & 1, c] = values[b]
            return 0

        lax.fori_loop(0, 3, scatter, 0)

        def one(slot, _):
            to = active_col(slot)
            mine = recv_c.at[j, :, :, pl.ds(KZS * col, KZS), :]

            @pl.when(to != col)
            def _():
                pltpu.make_async_remote_copy(
                    src_ref=send_c.at[j, slot],
                    dst_ref=mine,
                    send_sem=sc_sem,
                    recv_sem=rc_sem.at[j],
                    device_id={"col": to},
                    device_id_type=MESH,
                ).start()

            @pl.when(to == col)
            def _():
                pltpu.make_async_copy(send_c.at[j, slot], mine, rc_sem.at[j]).start()

            return 0

        lax.fori_loop(0, NCOL, one, 0)
        return 0

    lax.fori_loop(0, PARTS, stage_c, 0)

    for k in range(18):
        grad_part[k : k + 1, :] = jnp.sum(grad_acc[k], axis=0, keepdims=True)
    grad_part[18:24, :] = jnp.zeros((6, 128), F32)

    def share_row(k, _):
        pltpu.make_async_remote_copy(
            src_ref=grad_part,
            dst_ref=grad_row.at[row],
            send_sem=grad_send.at[0],
            recv_sem=grad_recv.at[0],
            device_id={"row": lax.rem(row + k, ROWS)},
            device_id_type=MESH,
        ).start()
        return 0

    lax.fori_loop(1, ROWS, share_row, 0)
    pltpu.make_async_copy(grad_part, grad_row.at[row], grad_recv.at[0]).start()

    loads[9].wait()

    def stage_d(j, _):
        @pl.when(col_active)
        def _():
            pltpu.make_async_copy(recv_c.at[j], recv_c.at[j], rc_sem.at[j]).wait()
            for c in range(3):
                for s in range(2):
                    high, low = split(recv_c[j, s, c])
                    rhs[256 * s : 256 * s + 256, 128 * c : 128 * c + 128] = high
                    rhs[512 + 256 * s : 768 + 256 * s, 128 * c : 128 * c + 128] = high
                    rhs[1024 + 256 * s : 1280 + 256 * s, 128 * c : 128 * c + 128] = low
            out = matmul(td[...], rhs[...])
            for slot in range(NROW):
                for t in range(2):
                    for c in range(3):
                        at = 64 * slot + 32 * t
                        send_d[j, slot, t, c] = out[at : at + 32, 128 * c : 128 * c + 128]

            def one(slot, _):
                to = active_row(slot)

                @pl.when(to != row)
                def _():
                    pltpu.make_async_remote_copy(
                        src_ref=send_d.at[j, slot],
                        dst_ref=arrived.at[row, j],
                        send_sem=sd_sem,
                        recv_sem=rd_sem,
                        device_id={"row": to},
                        device_id_type=MESH,
                    ).start()

                @pl.when(to == row)
                def _():
                    pltpu.make_async_copy(send_d.at[j, slot], arrived.at[row, j], rd_sem).start()

                return 0

            lax.fori_loop(0, NROW, one, 0)

        return 0

    lax.fori_loop(0, 2, stage_d, 0)

    pltpu.make_async_copy(grad_row, grad_row, grad_recv.at[0]).wait()
    grad_sum_row[...] = jnp.sum(grad_row[...], axis=0)

    def share_col(k, _):
        pltpu.make_async_remote_copy(
            src_ref=grad_sum_row,
            dst_ref=grad_col.at[col],
            send_sem=grad_send.at[1],
            recv_sem=grad_recv.at[1],
            device_id={"col": lax.rem(col + k, COLS)},
            device_id_type=MESH,
        ).start()
        return 0

    lax.fori_loop(1, COLS, share_col, 0)
    pltpu.make_async_copy(grad_sum_row, grad_col.at[col], grad_recv.at[1]).start()

    lax.fori_loop(2, 3, stage_d, 0)

    pltpu.make_async_copy(grad_col, grad_col, grad_recv.at[1]).wait()
    grad_sum_col[...] = jnp.sum(grad_col[...], axis=0)
    pltpu.make_async_remote_copy(
        src_ref=grad_sum_col,
        dst_ref=grad_env.at[env],
        send_sem=grad_send.at[2],
        recv_sem=grad_recv.at[2],
        device_id={"env": 1 - env},
        device_id_type=MESH,
    ).start()
    pltpu.make_async_copy(grad_sum_col, grad_env.at[env], grad_recv.at[2]).start()

    lax.fori_loop(3, 4, stage_d, 0)

    pltpu.make_async_copy(grad_env, grad_env, grad_recv.at[2]).wait()
    total = jnp.sum(grad_env[0] + grad_env[1], axis=1, keepdims=True)
    total = total * (1.0 / math.sqrt(2 * N**3))
    grad_out[...] = jnp.broadcast_to(total, (24, 128))

    for j in range(PARTS):
        sent_a = send_a.at[j, pl.ds(0, ROWS - 1)]
        pltpu.make_async_copy(sent_a, sent_a, sa_sem).wait()
        sent_b = recv_b.at[j, pl.ds(0, COLS - 1)]
        pltpu.make_async_copy(sent_b, sent_b, sb_sem).wait()

        @pl.when(col_active)
        def _():
            sent_c = send_c.at[j, pl.ds(0, NCOL - 1)]
            pltpu.make_async_copy(sent_c, sent_c, sc_sem).wait()

            @pl.when(row_active)
            def _():
                sent_d = send_d.at[j, pl.ds(0, NROW - 1)]
                pltpu.make_async_copy(sent_d, sent_d, sd_sem).wait()

            @pl.when(jnp.logical_not(row_active))
            def _():
                sent_d = send_d.at[j]
                pltpu.make_async_copy(sent_d, sent_d, sd_sem).wait()

        @pl.when(jnp.logical_not(col_active))
        def _():
            sent_c = send_c.at[j]
            pltpu.make_async_copy(sent_c, sent_c, sc_sem).wait()

    sent = grad_row.at[pl.ds(0, ROWS - 1)]
    pltpu.make_async_copy(sent, sent, grad_send.at[0]).wait()
    sent = grad_col.at[pl.ds(0, COLS - 1)]
    pltpu.make_async_copy(sent, sent, grad_send.at[1]).wait()
    sent = grad_env.at[0]
    pltpu.make_async_copy(sent, sent, grad_send.at[2]).wait()

    @pl.when(col_active & row_active)
    def _():
        pltpu.make_async_copy(arrived, arrived, rd_sem).wait()


def last_body(arrived, te, out, work, lhs, spec):
    row = lax.axis_index("row")
    col = lax.axis_index("col")
    tile = pl.program_id(0)
    active = ((col < 6) | (col >= 10)) & ((row < 3) | (row >= 5))

    @pl.when(jnp.logical_not(active))
    def _():
        out[...] = jnp.zeros_like(out)

    @pl.when(active)
    def _():
        def gather(step, _):
            c = step // 2
            s = step % 2
            for half in range(2):
                values = [arrived[slot & 7, 2 * half + (slot >> 3), s, c] for slot in range(16)]
                values = exchange(values, 1)
                at = pl.multiple_of(256 * s + 128 * half, 128)
                for kz in range(0, 16, 2):
                    high, low = split(jnp.concatenate((values[kz], values[kz + 1]), 0))
                    rows = pl.ds(pl.multiple_of(128 * c + 8 * kz, 16), 16)
                    lhs[rows, pl.ds(at, 128)] = high
                    lhs[rows, pl.ds(at + 512, 128)] = high
                    lhs[rows, pl.ds(at + 1024, 128)] = low
            return 0

        lax.fori_loop(0, 6, gather, 0)
        spec[...] = matmul(lhs[...], te[...])

        def signed(index):
            return jnp.where(index < N // 2, index, index - N).astype(F32)

        wave_x = signed(lax.broadcasted_iota(jnp.int32, (8, 256), 1))
        wave_y = signed(
            lax.broadcasted_iota(jnp.int32, (8, 256), 0) + (KYS * row + 8 * tile)
        )
        kept_xy = (3.0 * jnp.abs(wave_x) < N) & (3.0 * jnp.abs(wave_y) < N)
        square_xy = wave_x * wave_x + wave_y * wave_y

        def project(kz, _):
            wave_z = signed(jnp.full((8, 256), KZS * col + kz, jnp.int32))
            kept = kept_xy & (3.0 * jnp.abs(wave_z) < N)
            square = jnp.maximum(square_xy + wave_z * wave_z, 1.0)
            inverse = 1.0 / square
            waves = (wave_x, wave_y, wave_z)
            for t in range(2):
                parts = [
                    spec[
                        pl.ds(pl.multiple_of(128 * c + 8 * kz, 8), 8), 256 * t : 256 * t + 256
                    ]
                    for c in range(3)
                ]
                inner = (
                    wave_x * parts[0] + wave_y * parts[1] + wave_z * parts[2]
                ) * inverse
                for c in range(3):
                    value = jnp.where(kept, parts[c] - waves[c] * inner, 0.0)
                    for lanes in range(2):
                        work[c, t, lanes, pl.ds(kz, 8, stride=16), :] = value[
                            :, 128 * lanes : 128 * lanes + 128
                        ]
            return 0

        lax.fori_loop(0, 16, project, 0)
        for c in range(3):
            for t in range(2):
                for lanes in range(2):
                    out[c, t, :, 128 * lanes : 128 * lanes + 128] = work[c, t, lanes]


def shards(adjoint_hat, velocity, vorticity):
    table_a, table_b, table_c, table_z, table_d, table_e = (jnp.asarray(t) for t in tables())
    hbm = pl.BlockSpec(memory_space=pl.ANY)
    vmem = pltpu.VMEM
    dma = pltpu.SemaphoreType.DMA
    arrived, grad = pl.pallas_call(
        body,
        name="advect",
        out_shape=(
            jax.ShapeDtypeStruct((ROWS, PARTS, 2, 3, KYS, 128), F32),
            jax.ShapeDtypeStruct((24, 128), F32),
        ),
        in_specs=[hbm] * 8,
        out_specs=(hbm, pl.BlockSpec(memory_space=pltpu.VMEM)),
        scratch_shapes=[
            vmem((3, 2, 512, 256), F32),
            vmem((6, 512, 256), F32),
            vmem((2, 1536, 256), BF16),
            vmem((512, 1536), BF16),
            vmem((1536, 256), BF16),
            vmem((768, 384), BF16),
            vmem((384, 1536), BF16),
            vmem((3, 512, 1536), BF16),
            vmem((2, 512, 128), F32),
            vmem((PARTS, ROWS, 3, 2, KYS, 128), F32),
            vmem((PARTS, 3, 2, N, 128), F32),
            vmem((1536, 384), BF16),
            vmem((PARTS, 3, 2, N, 128), F32),
            vmem((PARTS, COLS, 3, 2, KZS, 128), F32),
            vmem((384, 1536), BF16),
            vmem((384, 256), F32),
            vmem((384, 768), BF16),
            vmem((384, 384), F32),
            vmem((PARTS, NCOL, 2, 3, KZS, 128), F32),
            vmem((PARTS, 2, 3, N, 128), F32),
            vmem((PARTS, NROW, 2, 3, KYS, 128), F32),
            vmem((18, 8, 128), F32),
            vmem((24, 128), F32),
            vmem((ROWS, 24, 128), F32),
            vmem((24, 128), F32),
            vmem((COLS, 24, 128), F32),
            vmem((24, 128), F32),
            vmem((2, 24, 128), F32),
            dma((10,)),
            dma((PARTS,)),
            dma((PARTS,)),
            dma((PARTS,)),
            dma,
            dma,
            dma,
            dma,
            dma,
            dma((3,)),
            dma((3,)),
        ],
        compiler_params=pltpu.CompilerParams(
            collective_id=0, has_side_effects=True, vmem_limit_bytes=60 * 2**20
        ),
    )(
        adjoint_hat.reshape(3, 2, 512, 256),
        velocity.reshape(3, 512, 256),
        vorticity.reshape(3, 512, 256),
        table_a, table_b, table_c, table_z, table_d,
    )
    out = pl.pallas_call(
        last_body,
        name="project",
        grid=(4,),
        out_shape=jax.ShapeDtypeStruct((3, 2, 512, 256), F32),
        in_specs=[
            pl.BlockSpec((ROWS, PARTS, 2, 3, 8, 128), lambda i: (0, 0, 0, 0, i, 0)),
            pl.BlockSpec((1536, 512), lambda i: (0, 0)),
        ],
        out_specs=pl.BlockSpec((3, 2, 128, 256), lambda i: (0, 0, i, 0)),
        scratch_shapes=[
            vmem((3, 2, 2, 128, 128), F32),
            vmem((384, 1536), BF16),
            vmem((384, 512), F32),
        ],
        compiler_params=pltpu.CompilerParams(vmem_limit_bytes=40 * 2**20),
    )(arrived, table_e)
    return out.reshape(adjoint_hat.shape), grad[:18, 0].reshape(3, 6)


def solution(mesh):
    placed = (
        P("env", None, None, "row", "col", None),
        P("env", None, "row", "col", None),
        P("env", None, "row", "col", None),
    )
    return jax.shard_map(
        shards,
        mesh=mesh,
        in_specs=placed,
        out_specs=(P("env", None, None, "row", "col", None), P()),
        check_vma=False,
    )
```

```python
import math

import jax
import jax.numpy as jnp
import ml_dtypes
import numpy as np
from jax import lax
from jax.experimental import pallas as pl
from jax.experimental.pallas import tpu as pltpu
from jax.sharding import PartitionSpec as P

F32 = jnp.float32
BF16 = jnp.bfloat16
MESH = pl.DeviceIdType.MESH

N = 256
ROWS = 8
COLS = 16
KYS = 32
KZS = 16
PARTS = 4
ACTIVE_COLS = (0, 1, 2, 3, 4, 5, 10, 11, 12, 13, 14, 15)
ACTIVE_ROWS = (0, 1, 2, 5, 6, 7)
NCOL = len(ACTIVE_COLS)
NROW = len(ACTIVE_ROWS)


def halves(table):
    high = table.astype(np.float32).astype(ml_dtypes.bfloat16)
    low = (table - high.astype(np.float64)).astype(np.float32).astype(ml_dtypes.bfloat16)
    return high, low


def stacked(table, axis):
    high, low = halves(table)
    return np.concatenate((high, low, high), axis)


def wave(out_index, in_index):
    angles = (np.outer(out_index, in_index) % N) * (2.0 * math.pi / N)
    return np.cos(angles) / math.sqrt(N), np.sin(angles) / math.sqrt(N)


def x_order():
    order = np.zeros((PARTS, ROWS, 8), np.int64)
    for part in range(PARTS):
        for row in range(ROWS):
            order[part, row] = 32 * row + 8 * part + np.arange(8)
    return order


def tables():
    every = np.arange(N)
    order = x_order()
    pieces = []
    for part in range(PARTS):
        cosines, sines = wave(order[part].reshape(-1), every)
        pieces.append(np.block([[cosines, -sines], [sines, cosines]]))
    table_a = stacked(np.concatenate(pieces, 0), 1)
    cosines, sines = wave(every, every)
    table_b = stacked(np.block([[cosines, -sines], [sines, cosines]]), 1)
    kz_order = np.arange(N).reshape(2, 8, KZS).transpose(0, 2, 1).reshape(-1)
    table_c = stacked(np.concatenate((cosines[kz_order], -sines[kz_order]), 0), 0)
    pieces = []
    for col in ACTIVE_COLS:
        kept = slice(KZS * col, KZS * col + KZS)
        pieces += [cosines[:, kept], -sines[:, kept]]
    table_z = stacked(np.concatenate(pieces, 1), 0)
    pieces = []
    for row in ACTIVE_ROWS:
        kept = slice(KYS * row, KYS * row + KYS)
        pieces.append(np.concatenate((cosines[kept], sines[kept]), 1))
        pieces.append(np.concatenate((-sines[kept], cosines[kept]), 1))
    table_d = stacked(np.concatenate(pieces, 0), 1)
    table_e = []
    for part in range(PARTS):
        block = np.zeros((8, 2, ROWS, 2, N))
        for row in range(ROWS):
            cosines, sines = wave(order[part, row], every)
            block[:, 0, row, 0], block[:, 0, row, 1] = cosines, -sines
            block[:, 1, row, 0], block[:, 1, row, 1] = sines, cosines
        table_e.append(stacked(block.reshape(128, 2 * N), 0))
    return table_a, table_b, table_c, table_z, table_d, np.stack(table_e)


def exchange(values, lane_bits):
    values = list(values)
    lane = lax.broadcasted_iota(jnp.int32, values[0].shape, 1)
    bit = 1
    while bit < len(values):
        step = bit * lane_bits
        clear = (lane & step) == 0
        for low in range(len(values)):
            if low & bit:
                continue
            first, second = values[low], values[low | bit]
            values[low] = jnp.where(clear, first, pltpu.roll(second, step, 1))
            values[low | bit] = jnp.where(clear, pltpu.roll(first, 128 - step, 1), second)
        bit *= 2
    return values


def split(value):
    high = value.astype(BF16)
    low = (value - high.astype(F32)).astype(BF16)
    return high, low


def matmul(left, right):
    return jnp.dot(left, right, preferred_element_type=F32)


def matmul_t(left, right):
    return lax.dot_general(
        left, right, (((1,), (1,)), ((), ())), preferred_element_type=F32
    )


def active_col(slot):
    return jnp.where(slot < 6, slot, slot + 4)


def active_row(slot):
    return jnp.where(slot < 3, slot, slot + 2)


def body(
    g_hbm, vel_hbm, vort_hbm, ta_hbm, tb_hbm, tc_hbm, tz_hbm, td_hbm, te_hbm,
    spec_out, grad_out,
    g, feat, ta, tb, tc, tz, td, te,
    data_a, send_a, recv_a, data_b, send_b, recv_b,
    lhs_c, work_c, lhs_z, work_z, send_c, recv_c, rhs, send_d, recv_d, lhs_e, spec,
    grad_acc, grad_part, grad_row, grad_sum_row, grad_col, grad_sum_col, grad_env,
    load_sem, ra_sem, rb_sem, rc_sem, rd_sem, sa_sem, sb_sem, sc_sem, sd_sem,
    grad_recv, grad_send, out_sem,
):
    env = lax.axis_index("env")
    row = lax.axis_index("row")
    col = lax.axis_index("col")
    col_active = (col < 6) | (col >= 10)
    row_active = (row < 3) | (row >= 5)

    barrier = pltpu.get_barrier_semaphore()

    def greet_row(k, _):
        pl.semaphore_signal(
            barrier, inc=1, device_id={"row": lax.rem(row + k, ROWS)}, device_id_type=MESH
        )
        return 0

    def greet_col(k, _):
        pl.semaphore_signal(
            barrier, inc=1, device_id={"col": lax.rem(col + k, COLS)}, device_id_type=MESH
        )
        return 0

    lax.fori_loop(1, ROWS, greet_row, 0)
    lax.fori_loop(1, COLS, greet_col, 0)
    pl.semaphore_signal(barrier, inc=1, device_id={"env": 1 - env}, device_id_type=MESH)

    def load_g(c):
        def one(kz, _):
            for s in range(2):
                pltpu.make_async_copy(
                    g_hbm.at[c, s, :, kz, :], g.at[c, s, kz], load_sem.at[1 + c]
                ).start()
            return 0

        lax.fori_loop(0, KZS, one, 0)

    loads = [pltpu.make_async_copy(ta_hbm, ta, load_sem.at[0])]
    for c in range(3):
        loads.append(pltpu.make_async_copy(g.at[c], g.at[c], load_sem.at[1 + c]))
    loads.append(pltpu.make_async_copy(tb_hbm, tb, load_sem.at[4]))
    loads.append(pltpu.make_async_copy(tc_hbm, tc, load_sem.at[5]))
    loads.append(pltpu.make_async_copy(vel_hbm, feat.at[pl.ds(0, 3)], load_sem.at[6]))
    loads.append(pltpu.make_async_copy(vort_hbm, feat.at[pl.ds(3, 3)], load_sem.at[7]))
    loads.append(pltpu.make_async_copy(tz_hbm, tz, load_sem.at[8]))
    loads.append(pltpu.make_async_copy(td_hbm, td, load_sem.at[9]))
    loads.append(pltpu.make_async_copy(te_hbm, te, load_sem.at[10]))
    load_g(0)
    loads[0].start()
    load_g(1)
    load_g(2)
    for load in loads[4:]:
        load.start()

    def start_row(c, j):
        def one(k, _):
            to = lax.rem(row + k, ROWS)
            pltpu.make_async_remote_copy(
                src_ref=send_a.at[c, j, to],
                dst_ref=recv_a.at[c, j, row],
                send_sem=sa_sem,
                recv_sem=ra_sem.at[c, j],
                device_id={"row": to},
                device_id_type=MESH,
            ).start()
            return 0

        lax.fori_loop(1, ROWS, one, 0)
        pltpu.make_async_copy(send_a.at[c, j, row], recv_a.at[c, j, row], ra_sem.at[c, j]).start()

    for c in range(3):
        loads[1 + c].wait()
        for s in range(2):
            high, low = split(g[c, s].reshape(512, 256))
            data_a[:, 256 * s : 256 * s + 256] = high
            data_a[:, 512 + 256 * s : 768 + 256 * s] = high
            data_a[:, 1024 + 256 * s : 1280 + 256 * s] = low
        if c == 0:
            loads[0].wait()
        for half in range(2):
            out = matmul_t(ta[256 * half : 256 * half + 256, :], data_a[...])
            for part in range(2):
                for t in range(2):
                    for r in range(ROWS):
                        at = 128 * part + 64 * t + 8 * r
                        for m in range(4):
                            send_a[c, 2 * half + part, r, t, m] = out[
                                at : at + 8, 128 * m : 128 * m + 128
                            ]
            if c == 0 and half == 0:
                pl.semaphore_wait(barrier, ROWS - 1 + COLS - 1 + 1)
            start_row(c, 2 * half)
            start_row(c, 2 * half + 1)

    loads[4].wait()

    def stage_b(unit, _):
        c = unit // PARTS
        j = unit % PARTS
        pltpu.make_async_copy(recv_a.at[c, j], recv_a.at[c, j], ra_sem.at[c, j]).wait()
        for t in range(2):
            for m in range(4):
                for group in range(2):
                    values = [recv_a[c, j, 4 * group + k, t, m] for k in range(4)]
                    values = exchange(values, 32)
                    at = 256 * t + 128 * group
                    for pair in range(2):
                        high, low = split(
                            jnp.concatenate((values[2 * pair], values[2 * pair + 1]), 0)
                        )
                        here = 32 * m + 16 * pair
                        data_b[here : here + 16, at : at + 128] = high
                        data_b[here : here + 16, at + 512 : at + 640] = high
                        data_b[here : here + 16, at + 1024 : at + 1152] = low
        out = matmul_t(tb[...], data_b[...])
        for t in range(2):
            send_b[c, j, t] = out[256 * t : 256 * t + 256, :]

        def one(k, _):
            to = lax.rem(col + k, COLS)
            pltpu.make_async_remote_copy(
                src_ref=send_b.at[c, j, :, pl.ds(KZS * to, KZS), :],
                dst_ref=recv_b.at[j, col, c],
                send_sem=sb_sem,
                recv_sem=rb_sem.at[j],
                device_id={"col": to},
                device_id_type=MESH,
            ).start()
            return 0

        lax.fori_loop(1, COLS, one, 0)
        pltpu.make_async_copy(
            send_b.at[c, j, :, pl.ds(KZS * col, KZS), :], recv_b.at[j, col, c], rb_sem.at[j]
        ).start()
        return 0

    lax.fori_loop(0, 3 * PARTS, stage_b, 0)

    for load in loads[5:]:
        load.wait()
    grad_acc[...] = jnp.zeros_like(grad_acc)

    def stage_c(j, _):
        pltpu.make_async_copy(recv_b.at[j], recv_b.at[j], rb_sem.at[j]).wait()

        def gather(step, _):
            c = step // 2
            s = step % 2
            for group in range(2):
                values = [recv_b[j, 8 * group + k, c, s] for k in range(8)]
                values = exchange(values, 1)
                at = pl.multiple_of(256 * s + 128 * group, 128)
                for x in range(8):
                    high, low = split(values[x])
                    rows = pl.ds(pl.multiple_of(128 * c + 16 * x, 16), 16)
                    lhs_c[rows, pl.ds(at, 128)] = high
                    lhs_c[rows, pl.ds(at + 512, 128)] = high
                    lhs_c[rows, pl.ds(at + 1024, 128)] = low
            return 0

        lax.fori_loop(0, 6, gather, 0)
        work_c[...] = matmul(lhs_c[...], tc[...])

        def cross(i, _):
            there = pl.ds(pl.multiple_of(128 * j + 16 * i, 16), 16)
            adjoint = [work_c[pl.ds(pl.multiple_of(128 * c + 16 * i, 16), 16), :] for c in range(3)]
            for f in range(6):
                feature = feat[f, there, :]
                for c in range(3):
                    product = adjoint[c] * feature
                    total = (product[:8, :128] + product[:8, 128:]) + (
                        product[8:, :128] + product[8:, 128:]
                    )
                    grad_acc[6 * c + f] += total
            spin = [feat[3 + c, there, :] for c in range(3)]
            for c in range(3):
                second, third = (c + 1) % 3, (c + 2) % 3
                high, low = split(
                    spin[second] * adjoint[third] - spin[third] * adjoint[second]
                )
                rows = pl.ds(pl.multiple_of(128 * c + 16 * i, 16), 16)
                lhs_z[rows, 0:256] = high
                lhs_z[rows, 256:512] = high
                lhs_z[rows, 512:768] = low
            return 0

        lax.fori_loop(0, 8, cross, 0)
        work_z[...] = matmul(lhs_z[...], tz[...])

        def scatter(c, _):
            for n in range(3):
                values = [
                    work_z[
                        pl.ds(pl.multiple_of(128 * c + 16 * x, 16), 16), 128 * n : 128 * n + 128
                    ]
                    for x in range(8)
                ]
                values = exchange(values, 16)
                for b in range(8):
                    block = 8 * n + b
                    send_c[j, c, block >> 1, block & 1] = values[b]

            def one(slot, _):
                to = active_col(slot)
                mine = recv_c.at[j, c, :, pl.ds(KZS * col, KZS), :]

                @pl.when(to != col)
                def _():
                    pltpu.make_async_remote_copy(
                        src_ref=send_c.at[j, c, slot],
                        dst_ref=mine,
                        send_sem=sc_sem,
                        recv_sem=rc_sem.at[j, c],
                        device_id={"col": to},
                        device_id_type=MESH,
                    ).start()

                @pl.when(to == col)
                def _():
                    pltpu.make_async_copy(send_c.at[j, c, slot], mine, rc_sem.at[j, c]).start()

                return 0

            lax.fori_loop(0, NCOL, one, 0)
            return 0

        lax.fori_loop(0, 3, scatter, 0)
        return 0

    lax.fori_loop(0, PARTS, stage_c, 0)

    for k in range(18):
        grad_part[k : k + 1, :] = jnp.sum(grad_acc[k], axis=0, keepdims=True)
    grad_part[18:24, :] = jnp.zeros((6, 128), F32)

    def share_row(k, _):
        pltpu.make_async_remote_copy(
            src_ref=grad_part,
            dst_ref=grad_row.at[row],
            send_sem=grad_send.at[0],
            recv_sem=grad_recv.at[0],
            device_id={"row": lax.rem(row + k, ROWS)},
            device_id_type=MESH,
        ).start()
        return 0

    lax.fori_loop(1, ROWS, share_row, 0)
    pltpu.make_async_copy(grad_part, grad_row.at[row], grad_recv.at[0]).start()

    def stage_d(unit, _):
        j = unit // 3
        c = unit % 3

        @pl.when(col_active)
        def _():
            pltpu.make_async_copy(recv_c.at[j, c], recv_c.at[j, c], rc_sem.at[j, c]).wait()
            for s in range(2):
                high, low = split(recv_c[j, c, s])
                rhs[256 * s : 256 * s + 256, :] = high
                rhs[512 + 256 * s : 768 + 256 * s, :] = high
                rhs[1024 + 256 * s : 1280 + 256 * s, :] = low
            out = matmul(td[...], rhs[...])
            for slot in range(NROW):
                for t in range(2):
                    at = 64 * slot + 32 * t
                    send_d[j, c, slot, t] = out[at : at + 32, :]

            def one(slot, _):
                to = active_row(slot)

                @pl.when(to != row)
                def _():
                    pltpu.make_async_remote_copy(
                        src_ref=send_d.at[j, c, slot],
                        dst_ref=recv_d.at[j, c, row],
                        send_sem=sd_sem,
                        recv_sem=rd_sem.at[j, c],
                        device_id={"row": to},
                        device_id_type=MESH,
                    ).start()

                @pl.when(to == row)
                def _():
                    pltpu.make_async_copy(
                        send_d.at[j, c, slot], recv_d.at[j, c, row], rd_sem.at[j, c]
                    ).start()

                return 0

            lax.fori_loop(0, NROW, one, 0)

        return 0

    def stage_e(unit, _):
        j = unit // 3
        c = unit % 3

        @pl.when(col_active & row_active)
        def _():
            pltpu.make_async_copy(recv_d.at[j, c], recv_d.at[j, c], rd_sem.at[j, c]).wait()

            def gather(step, _):
                at = pl.multiple_of(16 * step, 16)
                values = [
                    recv_d[j, c, k & 7, k >> 3, pl.ds(at, 16), :] for k in range(16)
                ]
                values = exchange(values, 1)
                for kz in range(16):
                    high, low = split(values[kz])
                    rows = pl.ds(pl.multiple_of(KYS * kz + at, 16), 16)
                    lhs_e[rows, 0:128] = high
                    lhs_e[rows, 128:256] = high
                    lhs_e[rows, 256:384] = low
                return 0

            lax.fori_loop(0, 2, gather, 0)

            @pl.when(j == 0)
            def _():
                spec[c] = matmul(lhs_e[...], te[j])

            @pl.when(j > 0)
            def _():
                spec[c] += matmul(lhs_e[...], te[j])

            @pl.when(j == PARTS - 1)
            def _():
                pltpu.make_async_copy(spec.at[c], spec_out.at[c], out_sem).start()

        return 0

    lax.fori_loop(0, 9, stage_d, 0)

    pltpu.make_async_copy(grad_row, grad_row, grad_recv.at[0]).wait()
    grad_sum_row[...] = jnp.sum(grad_row[...], axis=0)

    def share_col(k, _):
        pltpu.make_async_remote_copy(
            src_ref=grad_sum_row,
            dst_ref=grad_col.at[col],
            send_sem=grad_send.at[1],
            recv_sem=grad_recv.at[1],
            device_id={"col": lax.rem(col + k, COLS)},
            device_id_type=MESH,
        ).start()
        return 0

    lax.fori_loop(1, COLS, share_col, 0)
    pltpu.make_async_copy(grad_sum_row, grad_col.at[col], grad_recv.at[1]).start()

    lax.fori_loop(0, 9, stage_e, 0)

    pltpu.make_async_copy(grad_col, grad_col, grad_recv.at[1]).wait()
    grad_sum_col[...] = jnp.sum(grad_col[...], axis=0)
    pltpu.make_async_remote_copy(
        src_ref=grad_sum_col,
        dst_ref=grad_env.at[env],
        send_sem=grad_send.at[2],
        recv_sem=grad_recv.at[2],
        device_id={"env": 1 - env},
        device_id_type=MESH,
    ).start()
    pltpu.make_async_copy(grad_sum_col, grad_env.at[env], grad_recv.at[2]).start()

    lax.fori_loop(9, 12, stage_d, 0)

    pltpu.make_async_copy(grad_env, grad_env, grad_recv.at[2]).wait()
    total = jnp.sum(grad_env[0] + grad_env[1], axis=1, keepdims=True)
    total = total * (1.0 / math.sqrt(2 * N**3))
    grad_out[...] = jnp.broadcast_to(total, (24, 128))

    def sent(ref, sem):
        pltpu.make_async_copy(ref, ref, sem).wait()

    for j in range(PARTS):
        for c in range(3):
            sent(send_a.at[c, j, pl.ds(0, ROWS - 1)], sa_sem)
            sent(recv_b.at[j, pl.ds(0, COLS - 1), c], sb_sem)

    @pl.when(col_active)
    def _():
        for j in range(PARTS):
            for c in range(3):
                sent(send_c.at[j, c, pl.ds(0, NCOL - 1)], sc_sem)

    @pl.when(jnp.logical_not(col_active))
    def _():
        sent(send_c, sc_sem)

    sent(grad_row.at[pl.ds(0, ROWS - 1)], grad_send.at[0])
    sent(grad_col.at[pl.ds(0, COLS - 1)], grad_send.at[1])
    sent(grad_env.at[0], grad_send.at[2])

    lax.fori_loop(9, 12, stage_e, 0)

    @pl.when(col_active)
    def _():
        @pl.when(row_active)
        def _():
            for j in range(PARTS):
                for c in range(3):
                    sent(send_d.at[j, c, pl.ds(0, NROW - 1)], sd_sem)
            sent(spec, out_sem)

        @pl.when(jnp.logical_not(row_active))
        def _():
            sent(send_d, sd_sem)


def last_body(spec, out, work):
    row = lax.axis_index("row")
    col = lax.axis_index("col")
    tile = pl.program_id(0)
    active = ((col < 6) | (col >= 10)) & ((row < 3) | (row >= 5))

    @pl.when(jnp.logical_not(active))
    def _():
        out[...] = jnp.zeros_like(out)

    @pl.when(active)
    def _():
        def signed(index):
            return jnp.where(index < N // 2, index, index - N).astype(F32)

        wave_x = signed(lax.broadcasted_iota(jnp.int32, (8, 256), 1))
        wave_y = signed(
            lax.broadcasted_iota(jnp.int32, (8, 256), 0) + (KYS * row + 8 * tile)
        )
        kept_xy = (3.0 * jnp.abs(wave_x) < N) & (3.0 * jnp.abs(wave_y) < N)
        square_xy = wave_x * wave_x + wave_y * wave_y

        def project(kz, _):
            wave_z = signed(jnp.full((8, 256), KZS * col + kz, jnp.int32))
            kept = kept_xy & (3.0 * jnp.abs(wave_z) < N)
            square = jnp.maximum(square_xy + wave_z * wave_z, 1.0)
            inverse = 1.0 / square
            waves = (wave_x, wave_y, wave_z)
            for t in range(2):
                parts = [spec[c, kz, :, 256 * t : 256 * t + 256] for c in range(3)]
                inner = (
                    wave_x * parts[0] + wave_y * parts[1] + wave_z * parts[2]
                ) * inverse
                for c in range(3):
                    value = jnp.where(kept, parts[c] - waves[c] * inner, 0.0)
                    for lanes in range(2):
                        work[c, t, lanes, pl.ds(kz, 8, stride=16), :] = value[
                            :, 128 * lanes : 128 * lanes + 128
                        ]
            return 0

        lax.fori_loop(0, 16, project, 0)
        for c in range(3):
            for t in range(2):
                for lanes in range(2):
                    out[c, t, :, 128 * lanes : 128 * lanes + 128] = work[c, t, lanes]


def shards(adjoint_hat, velocity, vorticity):
    constants = [jnp.asarray(t) for t in tables()]
    hbm = pl.BlockSpec(memory_space=pl.ANY)
    vmem = pltpu.VMEM
    dma = pltpu.SemaphoreType.DMA
    spec, grad = pl.pallas_call(
        body,
        name="advect",
        out_shape=(
            jax.ShapeDtypeStruct((3, 512, 512), F32),
            jax.ShapeDtypeStruct((24, 128), F32),
        ),
        in_specs=[hbm] * 9,
        out_specs=(hbm, pl.BlockSpec(memory_space=pltpu.VMEM)),
        scratch_shapes=[
            vmem((3, 2, KZS, KYS, 256), F32),
            vmem((6, 512, 256), F32),
            vmem((512, 1536), BF16),
            vmem((512, 1536), BF16),
            vmem((1536, 256), BF16),
            vmem((768, 384), BF16),
            vmem((384, 1536), BF16),
            vmem((PARTS, 384, 512), BF16),
            vmem((512, 1536), BF16),
            vmem((3, PARTS, ROWS, 2, 4, 8, 128), F32),
            vmem((3, PARTS, ROWS, 2, 4, 8, 128), F32),
            vmem((128, 1536), BF16),
            vmem((3, PARTS, 2, N, 128), F32),
            vmem((PARTS, COLS, 3, 2, KZS, 128), F32),
            vmem((384, 1536), BF16),
            vmem((384, 256), F32),
            vmem((384, 768), BF16),
            vmem((384, 384), F32),
            vmem((PARTS, 3, NCOL, 2, KZS, 128), F32),
            vmem((PARTS, 3, 2, N, 128), F32),
            vmem((1536, 128), BF16),
            vmem((PARTS, 3, NROW, 2, KYS, 128), F32),
            vmem((PARTS, 3, ROWS, 2, KYS, 128), F32),
            vmem((512, 384), BF16),
            vmem((3, 512, 512), F32),
            vmem((18, 8, 128), F32),
            vmem((24, 128), F32),
            vmem((ROWS, 24, 128), F32),
            vmem((24, 128), F32),
            vmem((COLS, 24, 128), F32),
            vmem((24, 128), F32),
            vmem((2, 24, 128), F32),
            dma((11,)),
            dma((3, PARTS)),
            dma((PARTS,)),
            dma((PARTS, 3)),
            dma((PARTS, 3)),
            dma,
            dma,
            dma,
            dma,
            dma((3,)),
            dma((3,)),
            dma,
        ],
        compiler_params=pltpu.CompilerParams(
            collective_id=0, has_side_effects=True, vmem_limit_bytes=60 * 2**20
        ),
    )(
        adjoint_hat[0],
        velocity.reshape(3, 512, 256),
        vorticity.reshape(3, 512, 256),
        *constants,
    )
    out = pl.pallas_call(
        last_body,
        name="project",
        grid=(4,),
        out_shape=jax.ShapeDtypeStruct((3, 2, 512, 256), F32),
        in_specs=[pl.BlockSpec((3, KZS, 8, 512), lambda i: (0, 0, i, 0))],
        out_specs=pl.BlockSpec((3, 2, 128, 256), lambda i: (0, 0, i, 0)),
        scratch_shapes=[vmem((3, 2, 2, 128, 128), F32)],
        compiler_params=pltpu.CompilerParams(vmem_limit_bytes=40 * 2**20),
    )(spec.reshape(3, KZS, KYS, 512))
    return out.reshape(adjoint_hat.shape), grad[:18, 0].reshape(3, 6)


def solution(mesh):
    placed = (
        P("env", None, None, "row", "col", None),
        P("env", None, "row", "col", None),
        P("env", None, "row", "col", None),
    )
    return jax.shard_map(
        shards,
        mesh=mesh,
        in_specs=placed,
        out_specs=(P("env", None, None, "row", "col", None), P()),
        check_vma=False,
    )
```

```python
import math

import jax
import jax.numpy as jnp
import ml_dtypes
import numpy as np
from jax import lax
from jax.experimental import pallas as pl
from jax.experimental.pallas import tpu as pltpu
from jax.sharding import PartitionSpec as P

F32 = jnp.float32
BF16 = jnp.bfloat16
MESH = pl.DeviceIdType.MESH

N = 256
ROWS = 8
COLS = 16
KYS = 32
KZS = 16
PARTS = 4
WINDOW_B = 2
WINDOW_C = 2
ACTIVE_COLS = (0, 1, 2, 3, 4, 5, 10, 11, 12, 13, 14, 15)
ACTIVE_ROWS = (0, 1, 2, 5, 6, 7)
NCOL = len(ACTIVE_COLS)
NROW = len(ACTIVE_ROWS)


def halves(table):
    high = table.astype(np.float32).astype(ml_dtypes.bfloat16)
    low = (table - high.astype(np.float64)).astype(np.float32).astype(ml_dtypes.bfloat16)
    return high, low


def stacked(table, axis):
    high, low = halves(table)
    return np.concatenate((high, low, high), axis)


def wave(out_index, in_index):
    angles = (np.outer(out_index, in_index) % N) * (2.0 * math.pi / N)
    return np.cos(angles) / math.sqrt(N), np.sin(angles) / math.sqrt(N)


def x_order():
    order = np.zeros((PARTS, ROWS, 8), np.int64)
    for part in range(PARTS):
        for row in range(ROWS):
            order[part, row] = 32 * row + 8 * part + np.arange(8)
    return order


def tables():
    every = np.arange(N)
    order = x_order()
    pieces = []
    for part in range(PARTS):
        cosines, sines = wave(order[part].reshape(-1), every)
        pieces.append(np.block([[cosines, -sines], [sines, cosines]]))
    table_a = stacked(np.concatenate(pieces, 0), 1)
    cosines, sines = wave(every, every)
    table_b = stacked(np.block([[cosines, -sines], [sines, cosines]]), 1)
    kz_order = np.arange(N).reshape(2, 8, KZS).transpose(0, 2, 1).reshape(-1)
    table_c = stacked(np.concatenate((cosines[kz_order], -sines[kz_order]), 0), 0)
    pieces = []
    for col in ACTIVE_COLS:
        kept = slice(KZS * col, KZS * col + KZS)
        pieces += [cosines[:, kept], -sines[:, kept]]
    table_z = stacked(np.concatenate(pieces, 1), 0)
    pieces = []
    for row in ACTIVE_ROWS:
        kept = slice(KYS * row, KYS * row + KYS)
        pieces.append(np.concatenate((cosines[kept], sines[kept]), 1))
        pieces.append(np.concatenate((-sines[kept], cosines[kept]), 1))
    table_d = stacked(np.concatenate(pieces, 0), 1)
    table_e = []
    for part in range(PARTS):
        block = np.zeros((8, 2, ROWS, 2, N))
        for row in range(ROWS):
            cosines, sines = wave(order[part, row], every)
            block[:, 0, row, 0], block[:, 0, row, 1] = cosines, -sines
            block[:, 1, row, 0], block[:, 1, row, 1] = sines, cosines
        table_e.append(stacked(block.reshape(128, 2 * N), 0))
    return table_a, table_b, table_c, table_z, table_d, np.stack(table_e)


def exchange(values, lane_bits):
    values = list(values)
    lane = lax.broadcasted_iota(jnp.int32, values[0].shape, 1)
    bit = 1
    while bit < len(values):
        step = bit * lane_bits
        clear = (lane & step) == 0
        for low in range(len(values)):
            if low & bit:
                continue
            first, second = values[low], values[low | bit]
            values[low] = jnp.where(clear, first, pltpu.roll(second, step, 1))
            values[low | bit] = jnp.where(clear, pltpu.roll(first, 128 - step, 1), second)
        bit *= 2
    return values


def split(value):
    high = value.astype(BF16)
    low = (value - high.astype(F32)).astype(BF16)
    return high, low


def matmul(left, right):
    return jnp.dot(left, right, preferred_element_type=F32)


def matmul_t(left, right):
    return lax.dot_general(
        left, right, (((1,), (1,)), ((), ())), preferred_element_type=F32
    )


def offset(k, size):
    step = k
    away = step // 2 + 1
    return jnp.where(step % 2 == 0, away, size - away)


def is_active_col(col):
    return (col < 6) | (col >= 10)


def is_active_row(row):
    return (row < 3) | (row >= 5)


def body(
    g_hbm, vel_hbm, vort_hbm, ta_hbm, tb_hbm, tc_hbm, tz_hbm, td_hbm, te_hbm,
    spec_out, grad_out,
    g, feat, ta, tb, tc, tz, td, te,
    data_a, send_a, recv_a, data_b, send_b, recv_b,
    lhs_c, work_c, lhs_z, work_z, send_c, recv_c, rhs, send_d, recv_d, lhs_e, spec,
    grad_acc, grad_part, grad_row, grad_sum_row, grad_col, grad_sum_col, grad_env,
    load_sem, ra_sem, rb_sem, rc_sem, rd_sem, sa_sem, sb_sem, sc_sem, sd_sem,
    grad_recv, grad_send, out_sem,
):
    env = lax.axis_index("env")
    row = lax.axis_index("row")
    col = lax.axis_index("col")
    col_active = is_active_col(col)
    row_active = is_active_row(row)

    barrier = pltpu.get_barrier_semaphore()

    def greet_row(k, _):
        pl.semaphore_signal(
            barrier, inc=1, device_id={"row": lax.rem(row + k, ROWS)}, device_id_type=MESH
        )
        return 0

    def greet_col(k, _):
        pl.semaphore_signal(
            barrier, inc=1, device_id={"col": lax.rem(col + k, COLS)}, device_id_type=MESH
        )
        return 0

    lax.fori_loop(1, ROWS, greet_row, 0)
    lax.fori_loop(1, COLS, greet_col, 0)
    pl.semaphore_signal(barrier, inc=1, device_id={"env": 1 - env}, device_id_type=MESH)

    def load_g(c):
        def one(kz, _):
            pltpu.make_async_copy(
                g_hbm.at[c, :, :, kz, :], g.at[c, kz], load_sem.at[1 + c]
            ).start()
            return 0

        lax.fori_loop(0, KZS, one, 0)

    loads = [pltpu.make_async_copy(ta_hbm, ta, load_sem.at[0])]
    for c in range(3):
        loads.append(pltpu.make_async_copy(g.at[c], g.at[c], load_sem.at[1 + c]))
    loads.append(pltpu.make_async_copy(tb_hbm, tb, load_sem.at[4]))
    loads.append(pltpu.make_async_copy(tc_hbm, tc, load_sem.at[5]))
    loads.append(pltpu.make_async_copy(vel_hbm, feat.at[pl.ds(0, 3)], load_sem.at[6]))
    loads.append(pltpu.make_async_copy(vort_hbm, feat.at[pl.ds(3, 3)], load_sem.at[7]))
    loads.append(pltpu.make_async_copy(tz_hbm, tz, load_sem.at[8]))
    loads.append(pltpu.make_async_copy(td_hbm, td, load_sem.at[9]))
    loads.append(pltpu.make_async_copy(te_hbm, te, load_sem.at[10]))
    loads[0].start()
    load_g(0)
    loads[4].start()
    load_g(1)

    def start_row(c, j):
        def one(k, _):
            to = lax.rem(row + offset(k, ROWS), ROWS)
            pltpu.make_async_remote_copy(
                src_ref=send_a.at[c, j, to],
                dst_ref=recv_a.at[c, j, row],
                send_sem=sa_sem,
                recv_sem=ra_sem.at[c, j],
                device_id={"row": to},
                device_id_type=MESH,
            ).start()
            return 0

        lax.fori_loop(0, ROWS - 1, one, 0)
        pltpu.make_async_copy(send_a.at[c, j, row], recv_a.at[c, j, row], ra_sem.at[c, j]).start()

    for c in range(3):
        loads[1 + c].wait()
        for s in range(2):
            high, low = split(g[c, :, s].reshape(512, 256))
            data_a[:, 256 * s : 256 * s + 256] = high
            data_a[:, 512 + 256 * s : 768 + 256 * s] = high
            data_a[:, 1024 + 256 * s : 1280 + 256 * s] = low
        if c == 0:
            loads[0].wait()
        for half in range(2):
            out = matmul_t(ta[256 * half : 256 * half + 256, :], data_a[...])
            for part in range(2):
                for t in range(2):
                    for r in range(ROWS):
                        at = 128 * part + 64 * t + 8 * r
                        for m in range(4):
                            send_a[c, 2 * half + part, r, t, m] = out[
                                at : at + 8, 128 * m : 128 * m + 128
                            ]
            if c == 0 and half == 0:
                pl.semaphore_wait(barrier, ROWS - 1 + COLS - 1 + 1)
            start_row(c, 2 * half)
            start_row(c, 2 * half + 1)
        if c == 0:
            load_g(2)
            for load in loads[5:]:
                load.start()

    loads[4].wait()

    def sent(ref, sem):
        pltpu.make_async_copy(ref, ref, sem).wait()

    def sent_b(unit):
        sent(recv_b.at[0, pl.ds(0, COLS - 1), 0], sb_sem.at[unit])

    def sent_c(unit):
        @pl.when(col_active)
        def _():
            sent(send_c.at[0, 0, pl.ds(0, NCOL - 1)], sc_sem.at[unit])

        @pl.when(jnp.logical_not(col_active))
        def _():
            sent(send_c.at[0, 0], sc_sem.at[unit])

    def stage_b(unit, _):
        c = unit // PARTS
        j = unit % PARTS
        pltpu.make_async_copy(recv_a.at[c, j], recv_a.at[c, j], ra_sem.at[c, j]).wait()
        for t in range(2):
            for m in range(4):
                for group in range(2):
                    values = [recv_a[c, j, 4 * group + k, t, m] for k in range(4)]
                    values = exchange(values, 32)
                    at = 256 * t + 128 * group
                    for pair in range(2):
                        high, low = split(
                            jnp.concatenate((values[2 * pair], values[2 * pair + 1]), 0)
                        )
                        here = 32 * m + 16 * pair
                        data_b[here : here + 16, at : at + 128] = high
                        data_b[here : here + 16, at + 512 : at + 640] = high
                        data_b[here : here + 16, at + 1024 : at + 1152] = low
        out = matmul_t(tb[...], data_b[...])
        for t in range(2):
            send_b[c, j, t] = out[256 * t : 256 * t + 256, :]

        @pl.when(unit >= WINDOW_B)
        def _():
            sent_b(unit - WINDOW_B)

        def one(k, _):
            to = lax.rem(col + offset(k, COLS), COLS)
            pltpu.make_async_remote_copy(
                src_ref=send_b.at[c, j, :, pl.ds(KZS * to, KZS), :],
                dst_ref=recv_b.at[j, col, c],
                send_sem=sb_sem.at[unit],
                recv_sem=rb_sem.at[j],
                device_id={"col": to},
                device_id_type=MESH,
            ).start()
            return 0

        lax.fori_loop(0, COLS - 1, one, 0)
        pltpu.make_async_copy(
            send_b.at[c, j, :, pl.ds(KZS * col, KZS), :], recv_b.at[j, col, c], rb_sem.at[j]
        ).start()
        return 0

    lax.fori_loop(0, 3 * PARTS, stage_b, 0)

    for load in loads[5:]:
        load.wait()
    grad_acc[...] = jnp.zeros_like(grad_acc)

    def stage_c(j, _):
        pltpu.make_async_copy(recv_b.at[j], recv_b.at[j], rb_sem.at[j]).wait()

        def gather(step, _):
            c = step // 2
            s = step % 2
            for group in range(2):
                values = [recv_b[j, 8 * group + k, c, s] for k in range(8)]
                values = exchange(values, 1)
                at = pl.multiple_of(256 * s + 128 * group, 128)
                for x in range(8):
                    high, low = split(values[x])
                    rows = pl.ds(pl.multiple_of(128 * c + 16 * x, 16), 16)
                    lhs_c[rows, pl.ds(at, 128)] = high
                    lhs_c[rows, pl.ds(at + 512, 128)] = high
                    lhs_c[rows, pl.ds(at + 1024, 128)] = low
            return 0

        lax.fori_loop(0, 6, gather, 0)
        work_c[...] = matmul(lhs_c[...], tc[...])

        def cross(i, _):
            there = pl.ds(pl.multiple_of(128 * j + 16 * i, 16), 16)
            adjoint = [work_c[pl.ds(pl.multiple_of(128 * c + 16 * i, 16), 16), :] for c in range(3)]
            for f in range(6):
                feature = feat[f, there, :]
                for c in range(3):
                    product = adjoint[c] * feature
                    total = (product[:8, :128] + product[:8, 128:]) + (
                        product[8:, :128] + product[8:, 128:]
                    )
                    grad_acc[6 * c + f] += total
            spin = [feat[3 + c, there, :] for c in range(3)]
            for c in range(3):
                second, third = (c + 1) % 3, (c + 2) % 3
                high, low = split(
                    spin[second] * adjoint[third] - spin[third] * adjoint[second]
                )
                rows = pl.ds(pl.multiple_of(128 * c + 16 * i, 16), 16)
                lhs_z[rows, 0:256] = high
                lhs_z[rows, 256:512] = high
                lhs_z[rows, 512:768] = low
            return 0

        lax.fori_loop(0, 8, cross, 0)
        work_z[...] = matmul(lhs_z[...], tz[...])

        def scatter(c, _):
            for n in range(3):
                values = [
                    work_z[
                        pl.ds(pl.multiple_of(128 * c + 16 * x, 16), 16), 128 * n : 128 * n + 128
                    ]
                    for x in range(8)
                ]
                values = exchange(values, 16)
                for b in range(8):
                    block = 8 * n + b
                    send_c[j, c, block >> 1, block & 1] = values[b]

            unit = 3 * j + c

            @pl.when(unit >= WINDOW_C)
            def _():
                sent_c(unit - WINDOW_C)

            mine = recv_c.at[j, c, :, pl.ds(KZS * col, KZS), :]

            def one(k, _):
                to = lax.rem(col + offset(k, COLS), COLS)

                @pl.when(is_active_col(to))
                def _():
                    pltpu.make_async_remote_copy(
                        src_ref=send_c.at[j, c, jnp.where(to < 6, to, to - 4)],
                        dst_ref=mine,
                        send_sem=sc_sem.at[unit],
                        recv_sem=rc_sem.at[j, c],
                        device_id={"col": to},
                        device_id_type=MESH,
                    ).start()

                return 0

            lax.fori_loop(0, COLS - 1, one, 0)

            @pl.when(col_active)
            def _():
                own = send_c.at[j, c, jnp.where(col < 6, col, col - 4)]
                pltpu.make_async_copy(own, mine, rc_sem.at[j, c]).start()

            return 0

        lax.fori_loop(0, 3, scatter, 0)
        return 0

    def stage_d(unit, _):
        j = unit // 3
        c = unit % 3

        @pl.when(col_active)
        def _():
            pltpu.make_async_copy(recv_c.at[j, c], recv_c.at[j, c], rc_sem.at[j, c]).wait()
            for s in range(2):
                high, low = split(recv_c[j, c, s])
                rhs[256 * s : 256 * s + 256, :] = high
                rhs[512 + 256 * s : 768 + 256 * s, :] = high
                rhs[1024 + 256 * s : 1280 + 256 * s, :] = low
            out = matmul(td[...], rhs[...])
            for slot in range(NROW):
                for t in range(2):
                    at = 64 * slot + 32 * t
                    send_d[j, c, slot, t] = out[at : at + 32, :]

            mine = recv_d.at[j, c, row]

            def one(k, _):
                to = lax.rem(row + offset(k, ROWS), ROWS)

                @pl.when(is_active_row(to))
                def _():
                    pltpu.make_async_remote_copy(
                        src_ref=send_d.at[j, c, jnp.where(to < 3, to, to - 2)],
                        dst_ref=mine,
                        send_sem=sd_sem,
                        recv_sem=rd_sem.at[j, c],
                        device_id={"row": to},
                        device_id_type=MESH,
                    ).start()

                return 0

            lax.fori_loop(0, ROWS - 1, one, 0)

            @pl.when(row_active)
            def _():
                own = send_d.at[j, c, jnp.where(row < 3, row, row - 2)]
                pltpu.make_async_copy(own, mine, rd_sem.at[j, c]).start()

        return 0

    def stage_e(unit, _):
        j = unit // 3
        c = unit % 3

        @pl.when(col_active & row_active)
        def _():
            pltpu.make_async_copy(recv_d.at[j, c], recv_d.at[j, c], rd_sem.at[j, c]).wait()

            def gather(step, _):
                at = pl.multiple_of(16 * step, 16)
                values = [
                    recv_d[j, c, k & 7, k >> 3, pl.ds(at, 16), :] for k in range(16)
                ]
                values = exchange(values, 1)
                for kz in range(16):
                    high, low = split(values[kz])
                    rows = pl.ds(pl.multiple_of(KYS * kz + at, 16), 16)
                    lhs_e[rows, 0:128] = high
                    lhs_e[rows, 128:256] = high
                    lhs_e[rows, 256:384] = low
                return 0

            lax.fori_loop(0, 2, gather, 0)

            @pl.when(j == 0)
            def _():
                spec[c] = matmul(lhs_e[...], te[j])

            @pl.when(j > 0)
            def _():
                spec[c] += matmul(lhs_e[...], te[j])

            @pl.when(j == PARTS - 1)
            def _():
                pltpu.make_async_copy(spec.at[c], spec_out.at[c], out_sem).start()

        return 0

    stage_c(0, 0)
    stage_c(1, 0)
    lax.fori_loop(0, 3, stage_d, 0)
    stage_c(2, 0)
    lax.fori_loop(3, 6, stage_d, 0)
    lax.fori_loop(0, 3, stage_e, 0)
    stage_c(3, 0)

    for k in range(18):
        grad_part[k : k + 1, :] = jnp.sum(grad_acc[k], axis=0, keepdims=True)
    grad_part[18:24, :] = jnp.zeros((6, 128), F32)

    def share_row(k, _):
        pltpu.make_async_remote_copy(
            src_ref=grad_part,
            dst_ref=grad_row.at[row],
            send_sem=grad_send.at[0],
            recv_sem=grad_recv.at[0],
            device_id={"row": lax.rem(row + k, ROWS)},
            device_id_type=MESH,
        ).start()
        return 0

    lax.fori_loop(1, ROWS, share_row, 0)
    pltpu.make_async_copy(grad_part, grad_row.at[row], grad_recv.at[0]).start()

    lax.fori_loop(6, 9, stage_d, 0)
    lax.fori_loop(3, 6, stage_e, 0)

    pltpu.make_async_copy(grad_row, grad_row, grad_recv.at[0]).wait()
    grad_sum_row[...] = jnp.sum(grad_row[...], axis=0)

    def share_col(k, _):
        pltpu.make_async_remote_copy(
            src_ref=grad_sum_row,
            dst_ref=grad_col.at[col],
            send_sem=grad_send.at[1],
            recv_sem=grad_recv.at[1],
            device_id={"col": lax.rem(col + k, COLS)},
            device_id_type=MESH,
        ).start()
        return 0

    lax.fori_loop(1, COLS, share_col, 0)
    pltpu.make_async_copy(grad_sum_row, grad_col.at[col], grad_recv.at[1]).start()

    stage_d(9, 0)
    lax.fori_loop(6, 9, stage_e, 0)
    stage_d(10, 0)
    stage_e(9, 0)

    pltpu.make_async_copy(grad_col, grad_col, grad_recv.at[1]).wait()
    grad_sum_col[...] = jnp.sum(grad_col[...], axis=0)
    pltpu.make_async_remote_copy(
        src_ref=grad_sum_col,
        dst_ref=grad_env.at[env],
        send_sem=grad_send.at[2],
        recv_sem=grad_recv.at[2],
        device_id={"env": 1 - env},
        device_id_type=MESH,
    ).start()
    pltpu.make_async_copy(grad_sum_col, grad_env.at[env], grad_recv.at[2]).start()

    stage_d(11, 0)
    stage_e(10, 0)

    pltpu.make_async_copy(grad_env, grad_env, grad_recv.at[2]).wait()
    total = jnp.sum(grad_env[0] + grad_env[1], axis=1, keepdims=True)
    total = total * (1.0 / math.sqrt(2 * N**3))
    lane = lax.broadcasted_iota(jnp.int32, (1, 6), 1)
    for c in range(3):
        line = jnp.zeros((1, 6), F32)
        for f in range(6):
            line = jnp.where(lane == f, total[6 * c + f : 6 * c + f + 1, :], line)
        grad_out[c : c + 1, :] = line

    for c in range(3):
        for j in range(PARTS):
            sent(send_a.at[c, j, pl.ds(0, ROWS - 1)], sa_sem)
    for unit in range(3 * PARTS - WINDOW_B, 3 * PARTS):
        sent_b(unit)
    for unit in range(3 * PARTS - WINDOW_C, 3 * PARTS):
        sent_c(unit)
    sent(grad_row.at[pl.ds(0, ROWS - 1)], grad_send.at[0])
    sent(grad_col.at[pl.ds(0, COLS - 1)], grad_send.at[1])
    sent(grad_env.at[0], grad_send.at[2])

    stage_e(11, 0)

    @pl.when(col_active)
    def _():
        @pl.when(row_active)
        def _():
            for j in range(PARTS):
                for c in range(3):
                    sent(send_d.at[j, c, pl.ds(0, NROW - 1)], sd_sem)
            sent(spec, out_sem)

        @pl.when(jnp.logical_not(row_active))
        def _():
            sent(send_d, sd_sem)


def last_body(spec, sums, out, grad, before, after, in_sem, out_sem):
    row = lax.axis_index("row")
    col = lax.axis_index("col")
    active = is_active_col(col) & is_active_row(row)
    grad[...] = sums[...]

    def leave(kz, source):
        pltpu.make_async_copy(after.at[source], out.at[:, :, :, kz, :], out_sem).start()

    @pl.when(jnp.logical_not(active))
    def _():
        after[0] = jnp.zeros(after.shape[1:], F32)

        def one(kz, _):
            leave(kz, 0)
            return 0

        lax.fori_loop(0, KZS, one, 0)

    @pl.when(active)
    def _():
        def enter(kz, _):
            pltpu.make_async_copy(spec.at[:, kz], before.at[kz], in_sem.at[kz]).start()
            return 0

        lax.fori_loop(0, KZS, enter, 0)

        def signed(index):
            return jnp.where(index < N // 2, index, index - N).astype(F32)

        wave_x = signed(lax.broadcasted_iota(jnp.int32, (8, 256), 1))
        lines = lax.broadcasted_iota(jnp.int32, (8, 256), 0)

        def project(kz, _):
            pltpu.make_async_copy(before.at[kz], before.at[kz], in_sem.at[kz]).wait()
            wave_z = signed(jnp.full((8, 256), KZS * col + kz, jnp.int32))
            for tile in range(4):
                wave_y = signed(lines + (KYS * row + 8 * tile))
                kept = (
                    (3.0 * jnp.abs(wave_x) < N)
                    & (3.0 * jnp.abs(wave_y) < N)
                    & (3.0 * jnp.abs(wave_z) < N)
                )
                square = wave_x * wave_x + wave_y * wave_y + wave_z * wave_z
                inverse = 1.0 / jnp.maximum(square, 1.0)
                waves = (wave_x, wave_y, wave_z)
                here = slice(8 * tile, 8 * tile + 8)
                for t in range(2):
                    parts = [
                        before[kz, c, here, 256 * t : 256 * t + 256] for c in range(3)
                    ]
                    inner = (
                        wave_x * parts[0] + wave_y * parts[1] + wave_z * parts[2]
                    ) * inverse
                    for c in range(3):
                        after[kz, c, t, here, :] = jnp.where(
                            kept, parts[c] - waves[c] * inner, 0.0
                        )
            leave(kz, kz)
            return 0

        lax.fori_loop(0, KZS, project, 0)

    pltpu.make_async_copy(after, after, out_sem).wait()


def shards(adjoint_hat, velocity, vorticity):
    constants = [jnp.asarray(t) for t in tables()]
    hbm = pl.BlockSpec(memory_space=pl.ANY)
    vmem = pltpu.VMEM
    dma = pltpu.SemaphoreType.DMA
    spec, grad = pl.pallas_call(
        body,
        name="advect",
        out_shape=(
            jax.ShapeDtypeStruct((3, 512, 512), F32),
            jax.ShapeDtypeStruct((3, 6), F32),
        ),
        in_specs=[hbm] * 9,
        out_specs=(hbm, pl.BlockSpec(memory_space=pltpu.VMEM)),
        scratch_shapes=[
            vmem((3, KZS, 2, KYS, 256), F32),
            vmem((6, 512, 256), F32),
            vmem((512, 1536), BF16),
            vmem((512, 1536), BF16),
            vmem((1536, 256), BF16),
            vmem((768, 384), BF16),
            vmem((384, 1536), BF16),
            vmem((PARTS, 384, 512), BF16),
            vmem((512, 1536), BF16),
            vmem((3, PARTS, ROWS, 2, 4, 8, 128), F32),
            vmem((3, PARTS, ROWS, 2, 4, 8, 128), F32),
            vmem((128, 1536), BF16),
            vmem((3, PARTS, 2, N, 128), F32),
            vmem((PARTS, COLS, 3, 2, KZS, 128), F32),
            vmem((384, 1536), BF16),
            vmem((384, 256), F32),
            vmem((384, 768), BF16),
            vmem((384, 384), F32),
            vmem((PARTS, 3, NCOL, 2, KZS, 128), F32),
            vmem((PARTS, 3, 2, N, 128), F32),
            vmem((1536, 128), BF16),
            vmem((PARTS, 3, NROW, 2, KYS, 128), F32),
            vmem((PARTS, 3, ROWS, 2, KYS, 128), F32),
            vmem((512, 384), BF16),
            vmem((3, 512, 512), F32),
            vmem((18, 8, 128), F32),
            vmem((24, 128), F32),
            vmem((ROWS, 24, 128), F32),
            vmem((24, 128), F32),
            vmem((COLS, 24, 128), F32),
            vmem((24, 128), F32),
            vmem((2, 24, 128), F32),
            dma((11,)),
            dma((3, PARTS)),
            dma((PARTS,)),
            dma((PARTS, 3)),
            dma((PARTS, 3)),
            dma,
            dma((3 * PARTS,)),
            dma((3 * PARTS,)),
            dma,
            dma((3,)),
            dma((3,)),
            dma,
        ],
        compiler_params=pltpu.CompilerParams(
            collective_id=0, has_side_effects=True, vmem_limit_bytes=60 * 2**20
        ),
    )(
        adjoint_hat[0],
        velocity.reshape(3, 512, 256),
        vorticity.reshape(3, 512, 256),
        *constants,
    )
    out, grad = pl.pallas_call(
        last_body,
        name="project",
        out_shape=(
            jax.ShapeDtypeStruct((3, 2, KYS, KZS, N), F32),
            jax.ShapeDtypeStruct((3, 6), F32),
        ),
        in_specs=[hbm, pl.BlockSpec(memory_space=pltpu.VMEM)],
        out_specs=(hbm, pl.BlockSpec(memory_space=pltpu.VMEM)),
        scratch_shapes=[
            vmem((KZS, 3, KYS, 512), F32),
            vmem((KZS, 3, 2, KYS, N), F32),
            dma((KZS,)),
            dma,
        ],
        compiler_params=pltpu.CompilerParams(vmem_limit_bytes=60 * 2**20),
    )(spec.reshape(3, KZS, KYS, 512), grad)
    return out.reshape(adjoint_hat.shape), grad


def solution(mesh):
    placed = (
        P("env", None, None, "row", "col", None),
        P("env", None, "row", "col", None),
        P("env", None, "row", "col", None),
    )
    return jax.shard_map(
        shards,
        mesh=mesh,
        in_specs=placed,
        out_specs=(P("env", None, None, "row", "col", None), P()),
        check_vma=False,
    )
```

```python
import math

import jax
import jax.numpy as jnp
import ml_dtypes
import numpy as np
from jax import lax
from jax.experimental import pallas as pl
from jax.experimental.pallas import tpu as pltpu
from jax.sharding import PartitionSpec as P

F32 = jnp.float32
BF16 = jnp.bfloat16
MESH = pl.DeviceIdType.MESH

N = 256
ROWS = 8
COLS = 16
KYS = 32
KZS = 16
PARTS = 4
WINDOW_B = 2
WINDOW_C = 2
ACTIVE_COLS = (0, 1, 2, 3, 4, 5, 10, 11, 12, 13, 14, 15)
ACTIVE_ROWS = (0, 1, 2, 5, 6, 7)
NCOL = len(ACTIVE_COLS)
NROW = len(ACTIVE_ROWS)


def halves(table):
    high = table.astype(np.float32).astype(ml_dtypes.bfloat16)
    low = (table - high.astype(np.float64)).astype(np.float32).astype(ml_dtypes.bfloat16)
    return high, low


def stacked(table, axis):
    high, low = halves(table)
    return np.concatenate((high, low, high), axis)


def wave(out_index, in_index):
    angles = (np.outer(out_index, in_index) % N) * (2.0 * math.pi / N)
    return np.cos(angles) / math.sqrt(N), np.sin(angles) / math.sqrt(N)


def x_order():
    order = np.zeros((PARTS, ROWS, 8), np.int64)
    for part in range(PARTS):
        for row in range(ROWS):
            order[part, row] = 32 * row + 8 * part + np.arange(8)
    return order


def tables():
    every = np.arange(N)
    order = x_order()
    pieces = []
    for part in range(PARTS):
        cosines, sines = wave(order[part].reshape(-1), every)
        pieces.append(np.block([[cosines, -sines], [sines, cosines]]))
    table_a = stacked(np.concatenate(pieces, 0), 1)
    cosines, sines = wave(every, every)
    table_b = stacked(np.block([[cosines, -sines], [sines, cosines]]), 1)
    kz_order = np.arange(N).reshape(2, 8, KZS).transpose(0, 2, 1).reshape(-1)
    table_c = stacked(np.concatenate((cosines[kz_order], -sines[kz_order]), 0), 0)
    pieces = []
    for col in ACTIVE_COLS:
        kept = slice(KZS * col, KZS * col + KZS)
        pieces += [cosines[:, kept], -sines[:, kept]]
    table_z = stacked(np.concatenate(pieces, 1), 0)
    pieces = []
    for row in ACTIVE_ROWS:
        kept = slice(KYS * row, KYS * row + KYS)
        pieces.append(np.concatenate((cosines[kept], sines[kept]), 1))
        pieces.append(np.concatenate((-sines[kept], cosines[kept]), 1))
    table_d = stacked(np.concatenate(pieces, 0), 1)
    table_e = []
    for part in range(PARTS):
        block = np.zeros((8, 2, ROWS, 2, N))
        for row in range(ROWS):
            cosines, sines = wave(order[part, row], every)
            block[:, 0, row, 0], block[:, 0, row, 1] = cosines, -sines
            block[:, 1, row, 0], block[:, 1, row, 1] = sines, cosines
        table_e.append(stacked(block.reshape(128, 2 * N), 0))
    return table_a, table_b, table_c, table_z, table_d, np.stack(table_e)


def exchange(values, lane_bits):
    values = list(values)
    lane = lax.broadcasted_iota(jnp.int32, values[0].shape, 1)
    bit = 1
    while bit < len(values):
        step = bit * lane_bits
        clear = (lane & step) == 0
        for low in range(len(values)):
            if low & bit:
                continue
            first, second = values[low], values[low | bit]
            values[low] = jnp.where(clear, first, pltpu.roll(second, step, 1))
            values[low | bit] = jnp.where(clear, pltpu.roll(first, 128 - step, 1), second)
        bit *= 2
    return values


def split(value):
    high = value.astype(BF16)
    low = (value - high.astype(F32)).astype(BF16)
    return high, low


def matmul(left, right):
    return jnp.dot(left, right, preferred_element_type=F32)


def matmul_t(left, right):
    return lax.dot_general(
        left, right, (((1,), (1,)), ((), ())), preferred_element_type=F32
    )


def offset(k, size):
    step = k
    away = step // 2 + 1
    return jnp.where(step % 2 == 0, away, size - away)


def is_active_col(col):
    return (col < 6) | (col >= 10)


def is_active_row(row):
    return (row < 3) | (row >= 5)


def body(
    g_hbm, vel_hbm, vort_hbm, ta_hbm, tb_hbm, tc_hbm, tz_hbm, td_hbm, te_hbm,
    spec_out, grad_out,
    g, feat, ta, tb, tc, tz, td, te,
    data_a, send_a, recv_a, data_b, send_b, recv_b,
    lhs_c, work_c, lhs_z, work_z, send_c, recv_c, rhs, send_d, recv_d, lhs_e, spec,
    grad_acc, grad_part, grad_row, grad_sum_row, grad_col, grad_sum_col, grad_env,
    load_sem, ra_sem, rb_sem, rc_sem, rd_sem, sa_sem, sb_sem, sc_sem, sd_sem,
    grad_recv, grad_send, out_sem,
):
    env = lax.axis_index("env")
    row = lax.axis_index("row")
    col = lax.axis_index("col")
    col_active = is_active_col(col)
    row_active = is_active_row(row)

    def load_g(c):
        def one(kz, _):
            pltpu.make_async_copy(
                g_hbm.at[c, :, :, kz, :], g.at[c, kz], load_sem.at[1 + c]
            ).start()
            return 0

        lax.fori_loop(0, KZS, one, 0)

    half_a = pl.ds(0, 256)
    loads = [pltpu.make_async_copy(ta_hbm.at[half_a], ta.at[half_a], load_sem.at[0])]
    for c in range(3):
        loads.append(pltpu.make_async_copy(g.at[c], g.at[c], load_sem.at[1 + c]))
    loads.append(pltpu.make_async_copy(tb_hbm, tb, load_sem.at[4]))
    half_a = pl.ds(256, 256)
    loads.append(pltpu.make_async_copy(ta_hbm.at[half_a], ta.at[half_a], load_sem.at[11]))
    loads.append(pltpu.make_async_copy(tc_hbm, tc, load_sem.at[5]))
    loads.append(pltpu.make_async_copy(vel_hbm, feat.at[pl.ds(0, 3)], load_sem.at[6]))
    loads.append(pltpu.make_async_copy(vort_hbm, feat.at[pl.ds(3, 3)], load_sem.at[7]))
    loads.append(pltpu.make_async_copy(tz_hbm, tz, load_sem.at[8]))
    loads.append(pltpu.make_async_copy(td_hbm, td, load_sem.at[9]))
    loads.append(pltpu.make_async_copy(te_hbm, te, load_sem.at[10]))
    load_g(0)
    loads[0].start()
    barrier = pltpu.get_barrier_semaphore()

    def greet_row(k, _):
        pl.semaphore_signal(
            barrier, inc=1, device_id={"row": lax.rem(row + k, ROWS)}, device_id_type=MESH
        )
        return 0

    def greet_col(k, _):
        pl.semaphore_signal(
            barrier, inc=1, device_id={"col": lax.rem(col + k, COLS)}, device_id_type=MESH
        )
        return 0

    lax.fori_loop(1, ROWS, greet_row, 0)
    lax.fori_loop(1, COLS, greet_col, 0)
    pl.semaphore_signal(barrier, inc=1, device_id={"env": 1 - env}, device_id_type=MESH)

    load_g(1)
    loads[4].start()

    def start_row(c, j):
        def one(k, _):
            to = lax.rem(row + offset(k, ROWS), ROWS)
            pltpu.make_async_remote_copy(
                src_ref=send_a.at[c, j, to],
                dst_ref=recv_a.at[c, j, row],
                send_sem=sa_sem,
                recv_sem=ra_sem.at[c, j],
                device_id={"row": to},
                device_id_type=MESH,
            ).start()
            return 0

        lax.fori_loop(0, ROWS - 1, one, 0)
        pltpu.make_async_copy(send_a.at[c, j, row], recv_a.at[c, j, row], ra_sem.at[c, j]).start()

    def load_data(c):
        loads[1 + c].wait()
        for s in range(2):
            high, low = split(g[c, :, s].reshape(512, 256))
            data_a[:, 256 * s : 256 * s + 256] = high
            data_a[:, 512 + 256 * s : 768 + 256 * s] = high
            data_a[:, 1024 + 256 * s : 1280 + 256 * s] = low

    def stage_a(c, half):
        out = matmul_t(ta[256 * half : 256 * half + 256, :], data_a[...])
        for part in range(2):
            for t in range(2):
                for r in range(ROWS):
                    at = 128 * part + 64 * t + 8 * r
                    for m in range(4):
                        send_a[c, 2 * half + part, r, t, m] = out[
                            at : at + 8, 128 * m : 128 * m + 128
                        ]

    load_data(0)
    loads[0].wait()
    stage_a(0, 0)
    pl.semaphore_wait(barrier, ROWS - 1 + COLS - 1 + 1)
    start_row(0, 0)
    start_row(0, 1)
    loads[5].start()
    load_g(2)
    loads[5].wait()
    stage_a(0, 1)
    start_row(0, 2)
    start_row(0, 3)
    for load in loads[6:]:
        load.start()
    load_data(1)
    stage_a(1, 0)
    stage_a(1, 1)

    def sent(ref, sem):
        pltpu.make_async_copy(ref, ref, sem).wait()

    def sent_b(unit):
        sent(recv_b.at[0, pl.ds(0, COLS - 1), 0], sb_sem.at[unit])

    def sent_c(unit):
        @pl.when(col_active)
        def _():
            sent(send_c.at[0, 0, pl.ds(0, NCOL - 1)], sc_sem.at[unit])

        @pl.when(jnp.logical_not(col_active))
        def _():
            sent(send_c.at[0, 0], sc_sem.at[unit])

    def stage_b(unit, _):
        c = unit // PARTS
        j = unit % PARTS
        pltpu.make_async_copy(recv_a.at[c, j], recv_a.at[c, j], ra_sem.at[c, j]).wait()
        for t in range(2):
            for m in range(4):
                for group in range(2):
                    values = [recv_a[c, j, 4 * group + k, t, m] for k in range(4)]
                    values = exchange(values, 32)
                    at = 256 * t + 128 * group
                    for pair in range(2):
                        high, low = split(
                            jnp.concatenate((values[2 * pair], values[2 * pair + 1]), 0)
                        )
                        here = 32 * m + 16 * pair
                        data_b[here : here + 16, at : at + 128] = high
                        data_b[here : here + 16, at + 512 : at + 640] = high
                        data_b[here : here + 16, at + 1024 : at + 1152] = low
        out = matmul_t(tb[...], data_b[...])
        for t in range(2):
            send_b[c, j, t] = out[256 * t : 256 * t + 256, :]

        @pl.when(unit >= WINDOW_B)
        def _():
            sent_b(unit - WINDOW_B)

        def one(k, _):
            to = lax.rem(col + offset(k, COLS), COLS)
            pltpu.make_async_remote_copy(
                src_ref=send_b.at[c, j, :, pl.ds(KZS * to, KZS), :],
                dst_ref=recv_b.at[j, col, c],
                send_sem=sb_sem.at[unit],
                recv_sem=rb_sem.at[j],
                device_id={"col": to},
                device_id_type=MESH,
            ).start()
            return 0

        lax.fori_loop(0, COLS - 1, one, 0)
        pltpu.make_async_copy(
            send_b.at[c, j, :, pl.ds(KZS * col, KZS), :], recv_b.at[j, col, c], rb_sem.at[j]
        ).start()
        return 0

    loads[4].wait()
    stage_b(0, 0)
    for part in range(PARTS):
        start_row(1, part)
    stage_b(1, 0)
    load_data(2)
    stage_a(2, 0)
    stage_a(2, 1)
    for part in range(PARTS):
        start_row(2, part)
    lax.fori_loop(2, 3 * PARTS, stage_b, 0)

    for load in loads[6:]:
        load.wait()
    grad_acc[...] = jnp.zeros_like(grad_acc)

    def stage_d(unit, _):
        j = unit // 3
        c = unit % 3

        @pl.when(col_active)
        def _():
            pltpu.make_async_copy(recv_c.at[j, c], recv_c.at[j, c], rc_sem.at[j, c]).wait()
            for s in range(2):
                high, low = split(recv_c[j, c, s])
                rhs[256 * s : 256 * s + 256, :] = high
                rhs[512 + 256 * s : 768 + 256 * s, :] = high
                rhs[1024 + 256 * s : 1280 + 256 * s, :] = low
            out = matmul(td[...], rhs[...])
            for slot in range(NROW):
                for t in range(2):
                    at = 64 * slot + 32 * t
                    send_d[j, c, slot, t] = out[at : at + 32, :]

            mine = recv_d.at[j, c, row]

            def one(k, _):
                to = lax.rem(row + offset(k, ROWS), ROWS)

                @pl.when(is_active_row(to))
                def _():
                    pltpu.make_async_remote_copy(
                        src_ref=send_d.at[j, c, jnp.where(to < 3, to, to - 2)],
                        dst_ref=mine,
                        send_sem=sd_sem,
                        recv_sem=rd_sem.at[j, c],
                        device_id={"row": to},
                        device_id_type=MESH,
                    ).start()

                return 0

            lax.fori_loop(0, ROWS - 1, one, 0)

            @pl.when(row_active)
            def _():
                own = send_d.at[j, c, jnp.where(row < 3, row, row - 2)]
                pltpu.make_async_copy(own, mine, rd_sem.at[j, c]).start()

        return 0

    def stage_e(unit, _):
        j = unit // 3
        c = unit % 3

        @pl.when(col_active & row_active)
        def _():
            pltpu.make_async_copy(recv_d.at[j, c], recv_d.at[j, c], rd_sem.at[j, c]).wait()

            def gather(step, _):
                at = pl.multiple_of(16 * step, 16)
                values = [
                    recv_d[j, c, k & 7, k >> 3, pl.ds(at, 16), :] for k in range(16)
                ]
                values = exchange(values, 1)
                for kz in range(16):
                    high, low = split(values[kz])
                    rows = pl.ds(pl.multiple_of(KYS * kz + at, 16), 16)
                    lhs_e[rows, 0:128] = high
                    lhs_e[rows, 128:256] = high
                    lhs_e[rows, 256:384] = low
                return 0

            lax.fori_loop(0, 2, gather, 0)

            @pl.when(j == 0)
            def _():
                spec[c] = matmul(lhs_e[...], te[j])

            @pl.when(j > 0)
            def _():
                spec[c] += matmul(lhs_e[...], te[j])

            @pl.when(j == PARTS - 1)
            def _():
                pltpu.make_async_copy(spec.at[c], spec_out.at[c], out_sem).start()

        return 0

    def stage_c(j, _):
        pltpu.make_async_copy(recv_b.at[j], recv_b.at[j], rb_sem.at[j]).wait()

        def gather(step, _):
            c = step // 2
            s = step % 2
            for group in range(2):
                values = [recv_b[j, 8 * group + k, c, s] for k in range(8)]
                values = exchange(values, 1)
                at = pl.multiple_of(256 * s + 128 * group, 128)
                for x in range(8):
                    high, low = split(values[x])
                    rows = pl.ds(pl.multiple_of(128 * c + 16 * x, 16), 16)
                    lhs_c[rows, pl.ds(at, 128)] = high
                    lhs_c[rows, pl.ds(at + 512, 128)] = high
                    lhs_c[rows, pl.ds(at + 1024, 128)] = low
            return 0

        lax.fori_loop(0, 6, gather, 0)
        work_c[...] = matmul(lhs_c[...], tc[...])

        def cross(i, _):
            there = pl.ds(pl.multiple_of(128 * j + 16 * i, 16), 16)
            adjoint = [work_c[pl.ds(pl.multiple_of(128 * c + 16 * i, 16), 16), :] for c in range(3)]
            for f in range(6):
                feature = feat[f, there, :]
                for c in range(3):
                    product = adjoint[c] * feature
                    total = (product[:8, :128] + product[:8, 128:]) + (
                        product[8:, :128] + product[8:, 128:]
                    )
                    grad_acc[6 * c + f] += total
            spin = [feat[3 + c, there, :] for c in range(3)]
            for c in range(3):
                second, third = (c + 1) % 3, (c + 2) % 3
                high, low = split(
                    spin[second] * adjoint[third] - spin[third] * adjoint[second]
                )
                rows = pl.ds(pl.multiple_of(128 * c + 16 * i, 16), 16)
                lhs_z[rows, 0:256] = high
                lhs_z[rows, 256:512] = high
                lhs_z[rows, 512:768] = low
            return 0

        lax.fori_loop(0, 8, cross, 0)
        work_z[...] = matmul(lhs_z[...], tz[...])

        def scatter(c, _):
            for n in range(3):
                values = [
                    work_z[
                        pl.ds(pl.multiple_of(128 * c + 16 * x, 16), 16), 128 * n : 128 * n + 128
                    ]
                    for x in range(8)
                ]
                values = exchange(values, 16)
                for b in range(8):
                    block = 8 * n + b
                    send_c[j, c, block >> 1, block & 1] = values[b]

            unit = 3 * j + c

            @pl.when(unit >= WINDOW_C)
            def _():
                sent_c(unit - WINDOW_C)

            mine = recv_c.at[j, c, :, pl.ds(KZS * col, KZS), :]

            def one(k, _):
                to = lax.rem(col + offset(k, COLS), COLS)

                @pl.when(is_active_col(to))
                def _():
                    pltpu.make_async_remote_copy(
                        src_ref=send_c.at[j, c, jnp.where(to < 6, to, to - 4)],
                        dst_ref=mine,
                        send_sem=sc_sem.at[unit],
                        recv_sem=rc_sem.at[j, c],
                        device_id={"col": to},
                        device_id_type=MESH,
                    ).start()

                return 0

            lax.fori_loop(0, COLS - 1, one, 0)

            @pl.when(col_active)
            def _():
                own = send_c.at[j, c, jnp.where(col < 6, col, col - 4)]
                pltpu.make_async_copy(own, mine, rc_sem.at[j, c]).start()

            return 0

        lax.fori_loop(0, 3, scatter, 0)
        return 0

    stage_c(0, 0)
    stage_c(1, 0)
    lax.fori_loop(0, 3, stage_d, 0)
    stage_c(2, 0)
    lax.fori_loop(3, 6, stage_d, 0)
    lax.fori_loop(0, 3, stage_e, 0)
    stage_c(3, 0)

    for k in range(18):
        grad_part[k : k + 1, :] = jnp.sum(grad_acc[k], axis=0, keepdims=True)
    grad_part[18:24, :] = jnp.zeros((6, 128), F32)

    def share_row(k, _):
        pltpu.make_async_remote_copy(
            src_ref=grad_part,
            dst_ref=grad_row.at[row],
            send_sem=grad_send.at[0],
            recv_sem=grad_recv.at[0],
            device_id={"row": lax.rem(row + k, ROWS)},
            device_id_type=MESH,
        ).start()
        return 0

    lax.fori_loop(1, ROWS, share_row, 0)
    pltpu.make_async_copy(grad_part, grad_row.at[row], grad_recv.at[0]).start()

    sent(send_a.at[:, :, pl.ds(0, ROWS - 1)], sa_sem)
    for unit in range(3 * PARTS - WINDOW_B, 3 * PARTS):
        sent_b(unit)

    lax.fori_loop(6, 9, stage_d, 0)
    lax.fori_loop(3, 6, stage_e, 0)
    stage_d(9, 0)
    lax.fori_loop(6, 8, stage_e, 0)
    stage_d(10, 0)
    pltpu.make_async_copy(grad_row, grad_row, grad_recv.at[0]).wait()
    grad_sum_row[...] = jnp.sum(grad_row[...], axis=0)

    def share_col(k, _):
        pltpu.make_async_remote_copy(
            src_ref=grad_sum_row,
            dst_ref=grad_col.at[col],
            send_sem=grad_send.at[1],
            recv_sem=grad_recv.at[1],
            device_id={"col": lax.rem(col + k, COLS)},
            device_id_type=MESH,
        ).start()
        return 0

    lax.fori_loop(1, COLS, share_col, 0)
    pltpu.make_async_copy(grad_sum_row, grad_col.at[col], grad_recv.at[1]).start()

    stage_e(8, 0)
    stage_d(11, 0)
    pltpu.make_async_copy(grad_col, grad_col, grad_recv.at[1]).wait()
    grad_sum_col[...] = jnp.sum(grad_col[...], axis=0)
    pltpu.make_async_remote_copy(
        src_ref=grad_sum_col,
        dst_ref=grad_env.at[env],
        send_sem=grad_send.at[2],
        recv_sem=grad_recv.at[2],
        device_id={"env": 1 - env},
        device_id_type=MESH,
    ).start()
    pltpu.make_async_copy(grad_sum_col, grad_env.at[env], grad_recv.at[2]).start()

    stage_e(9, 0)
    stage_e(10, 0)
    pltpu.make_async_copy(grad_env, grad_env, grad_recv.at[2]).wait()
    total = jnp.sum(grad_env[0] + grad_env[1], axis=1, keepdims=True)
    total = total * (1.0 / math.sqrt(2 * N**3))
    lane = lax.broadcasted_iota(jnp.int32, (1, 6), 1)
    for c in range(3):
        line = jnp.zeros((1, 6), F32)
        for f in range(6):
            line = jnp.where(lane == f, total[6 * c + f : 6 * c + f + 1, :], line)
        grad_out[c : c + 1, :] = line

    for unit in range(3 * PARTS - WINDOW_C, 3 * PARTS):
        sent_c(unit)
    sent(grad_row.at[pl.ds(0, ROWS - 1)], grad_send.at[0])
    sent(grad_col.at[pl.ds(0, COLS - 1)], grad_send.at[1])
    sent(grad_env.at[0], grad_send.at[2])

    stage_e(11, 0)

    @pl.when(col_active)
    def _():
        @pl.when(row_active)
        def _():
            sent(send_d.at[:, :, pl.ds(0, NROW - 1)], sd_sem)
            sent(spec, out_sem)

        @pl.when(jnp.logical_not(row_active))
        def _():
            sent(send_d, sd_sem)


def last_body(spec, sums, out, grad, before, after, in_sem, out_sem):
    row = lax.axis_index("row")
    col = lax.axis_index("col")
    active = is_active_col(col) & is_active_row(row)
    grad[...] = sums[...]

    def leave(kz, source):
        pltpu.make_async_copy(after.at[source], out.at[:, :, :, kz, :], out_sem).start()

    @pl.when(jnp.logical_not(active))
    def _():
        after[0] = jnp.zeros(after.shape[1:], F32)

        def one(kz, _):
            leave(kz, 0)
            return 0

        lax.fori_loop(0, KZS, one, 0)

    @pl.when(active)
    def _():
        def enter(kz, _):
            pltpu.make_async_copy(spec.at[:, kz], before.at[kz], in_sem.at[kz]).start()
            return 0

        lax.fori_loop(0, KZS, enter, 0)

        def signed(index):
            return jnp.where(index < N // 2, index, index - N).astype(F32)

        wave_x = signed(lax.broadcasted_iota(jnp.int32, (8, 256), 1))
        lines = lax.broadcasted_iota(jnp.int32, (8, 256), 0)

        def project(kz, _):
            pltpu.make_async_copy(before.at[kz], before.at[kz], in_sem.at[kz]).wait()
            wave_z = signed(jnp.full((8, 256), KZS * col + kz, jnp.int32))
            for tile in range(4):
                wave_y = signed(lines + (KYS * row + 8 * tile))
                kept = (
                    (3.0 * jnp.abs(wave_x) < N)
                    & (3.0 * jnp.abs(wave_y) < N)
                    & (3.0 * jnp.abs(wave_z) < N)
                )
                square = wave_x * wave_x + wave_y * wave_y + wave_z * wave_z
                inverse = 1.0 / jnp.maximum(square, 1.0)
                waves = (wave_x, wave_y, wave_z)
                here = slice(8 * tile, 8 * tile + 8)
                for t in range(2):
                    parts = [
                        before[kz, c, here, 256 * t : 256 * t + 256] for c in range(3)
                    ]
                    inner = (
                        wave_x * parts[0] + wave_y * parts[1] + wave_z * parts[2]
                    ) * inverse
                    for c in range(3):
                        after[kz, c, t, here, :] = jnp.where(
                            kept, parts[c] - waves[c] * inner, 0.0
                        )
            leave(kz, kz)
            return 0

        lax.fori_loop(0, KZS, project, 0)

    pltpu.make_async_copy(after, after, out_sem).wait()


def shards(adjoint_hat, velocity, vorticity):
    constants = [jnp.asarray(t) for t in tables()]
    hbm = pl.BlockSpec(memory_space=pl.ANY)
    vmem = pltpu.VMEM
    dma = pltpu.SemaphoreType.DMA
    spec, grad = pl.pallas_call(
        body,
        name="advect",
        out_shape=(
            jax.ShapeDtypeStruct((3, 512, 512), F32),
            jax.ShapeDtypeStruct((3, 6), F32),
        ),
        in_specs=[hbm] * 9,
        out_specs=(hbm, pl.BlockSpec(memory_space=pltpu.VMEM)),
        scratch_shapes=[
            vmem((3, KZS, 2, KYS, 256), F32),
            vmem((6, 512, 256), F32),
            vmem((512, 1536), BF16),
            vmem((512, 1536), BF16),
            vmem((1536, 256), BF16),
            vmem((768, 384), BF16),
            vmem((384, 1536), BF16),
            vmem((PARTS, 384, 512), BF16),
            vmem((512, 1536), BF16),
            vmem((3, PARTS, ROWS, 2, 4, 8, 128), F32),
            vmem((3, PARTS, ROWS, 2, 4, 8, 128), F32),
            vmem((128, 1536), BF16),
            vmem((3, PARTS, 2, N, 128), F32),
            vmem((PARTS, COLS, 3, 2, KZS, 128), F32),
            vmem((384, 1536), BF16),
            vmem((384, 256), F32),
            vmem((384, 768), BF16),
            vmem((384, 384), F32),
            vmem((PARTS, 3, NCOL, 2, KZS, 128), F32),
            vmem((PARTS, 3, 2, N, 128), F32),
            vmem((1536, 128), BF16),
            vmem((PARTS, 3, NROW, 2, KYS, 128), F32),
            vmem((PARTS, 3, ROWS, 2, KYS, 128), F32),
            vmem((512, 384), BF16),
            vmem((3, 512, 512), F32),
            vmem((18, 8, 128), F32),
            vmem((24, 128), F32),
            vmem((ROWS, 24, 128), F32),
            vmem((24, 128), F32),
            vmem((COLS, 24, 128), F32),
            vmem((24, 128), F32),
            vmem((2, 24, 128), F32),
            dma((12,)),
            dma((3, PARTS)),
            dma((PARTS,)),
            dma((PARTS, 3)),
            dma((PARTS, 3)),
            dma,
            dma((3 * PARTS,)),
            dma((3 * PARTS,)),
            dma,
            dma((3,)),
            dma((3,)),
            dma,
        ],
        compiler_params=pltpu.CompilerParams(
            collective_id=0, has_side_effects=True, vmem_limit_bytes=60 * 2**20
        ),
    )(
        adjoint_hat[0],
        velocity.reshape(3, 512, 256),
        vorticity.reshape(3, 512, 256),
        *constants,
    )
    out, grad = pl.pallas_call(
        last_body,
        name="project",
        out_shape=(
            jax.ShapeDtypeStruct((3, 2, KYS, KZS, N), F32),
            jax.ShapeDtypeStruct((3, 6), F32),
        ),
        in_specs=[hbm, pl.BlockSpec(memory_space=pltpu.VMEM)],
        out_specs=(hbm, pl.BlockSpec(memory_space=pltpu.VMEM)),
        scratch_shapes=[
            vmem((KZS, 3, KYS, 512), F32),
            vmem((KZS, 3, 2, KYS, N), F32),
            dma((KZS,)),
            dma,
        ],
        compiler_params=pltpu.CompilerParams(vmem_limit_bytes=60 * 2**20),
    )(spec.reshape(3, KZS, KYS, 512), grad)
    return out.reshape(adjoint_hat.shape), grad


def solution(mesh):
    placed = (
        P("env", None, None, "row", "col", None),
        P("env", None, "row", "col", None),
        P("env", None, "row", "col", None),
    )
    return jax.shard_map(
        shards,
        mesh=mesh,
        in_specs=placed,
        out_specs=(P("env", None, None, "row", "col", None), P()),
        check_vma=False,
    )
```

```python
import math

import jax
import jax.numpy as jnp
import ml_dtypes
import numpy as np
from jax import lax
from jax.experimental import pallas as pl
from jax.experimental.pallas import tpu as pltpu
from jax.sharding import PartitionSpec as P

F32 = jnp.float32
BF16 = jnp.bfloat16
MESH = pl.DeviceIdType.MESH

N = 256
ROWS = 8
COLS = 16
KYS = 32
KZS = 16
PARTS = 4
TILES = 8
WINDOW_B = 2
WINDOW_C = 2
ACTIVE_COLS = (0, 1, 2, 3, 4, 5, 10, 11, 12, 13, 14, 15)
ACTIVE_ROWS = (0, 1, 2, 5, 6, 7)
NCOL = len(ACTIVE_COLS)
NROW = len(ACTIVE_ROWS)


def halves(table):
    high = table.astype(np.float32).astype(ml_dtypes.bfloat16)
    low = (table - high.astype(np.float64)).astype(np.float32).astype(ml_dtypes.bfloat16)
    return high, low


def stacked(table, axis):
    high, low = halves(table)
    return np.concatenate((high, low, high), axis)


def wave(out_index, in_index):
    angles = (np.outer(out_index, in_index) % N) * (2.0 * math.pi / N)
    return np.cos(angles) / math.sqrt(N), np.sin(angles) / math.sqrt(N)


def x_order():
    order = np.zeros((PARTS, ROWS, 8), np.int64)
    for part in range(PARTS):
        for row in range(ROWS):
            order[part, row] = 32 * row + 8 * part + np.arange(8)
    return order


def tables():
    every = np.arange(N)
    order = x_order()
    pieces = []
    for part in range(PARTS):
        cosines, sines = wave(order[part].reshape(-1), every)
        pieces.append(np.block([[cosines, -sines], [sines, cosines]]))
    table_a = stacked(np.concatenate(pieces, 0), 1)
    cosines, sines = wave(every, every)
    table_b = stacked(np.block([[cosines, -sines], [sines, cosines]]), 1)
    kz_order = np.arange(N).reshape(2, 8, KZS).transpose(0, 2, 1).reshape(-1)
    table_c = stacked(np.concatenate((cosines[kz_order], -sines[kz_order]), 0), 0)
    pieces = []
    for col in ACTIVE_COLS:
        kept = slice(KZS * col, KZS * col + KZS)
        pieces += [cosines[:, kept], -sines[:, kept]]
    table_z = stacked(np.concatenate(pieces, 1), 0)
    pieces = []
    for row in ACTIVE_ROWS:
        kept = slice(KYS * row, KYS * row + KYS)
        pieces.append(np.concatenate((cosines[kept], sines[kept]), 1))
        pieces.append(np.concatenate((-sines[kept], cosines[kept]), 1))
    table_d = stacked(np.concatenate(pieces, 0), 1)
    table_e = []
    for part in range(PARTS):
        block = np.zeros((8, 2, ROWS, 2, N))
        for row in range(ROWS):
            cosines, sines = wave(order[part, row], every)
            block[:, 0, row, 0], block[:, 0, row, 1] = cosines, -sines
            block[:, 1, row, 0], block[:, 1, row, 1] = sines, cosines
        table_e.append(stacked(block.reshape(128, 2 * N), 0))
    return table_a, table_b, table_c, table_z, table_d, np.stack(table_e)


def exchange(values, lane_bits):
    values = list(values)
    lane = lax.broadcasted_iota(jnp.int32, values[0].shape, 1)
    bit = 1
    while bit < len(values):
        step = bit * lane_bits
        clear = (lane & step) == 0
        for low in range(len(values)):
            if low & bit:
                continue
            first, second = values[low], values[low | bit]
            values[low] = jnp.where(clear, first, pltpu.roll(second, step, 1))
            values[low | bit] = jnp.where(clear, pltpu.roll(first, 128 - step, 1), second)
        bit *= 2
    return values


def split(value):
    high = value.astype(BF16)
    low = (value - high.astype(F32)).astype(BF16)
    return high, low


def matmul(left, right):
    return jnp.dot(left, right, preferred_element_type=F32)


def matmul_t(left, right):
    return lax.dot_general(
        left, right, (((1,), (1,)), ((), ())), preferred_element_type=F32
    )


def offset(k, size):
    step = k
    away = step // 2 + 1
    return jnp.where(step % 2 == 0, away, size - away)


def is_active_col(col):
    return (col < 6) | (col >= 10)


def is_active_row(row):
    return (row < 3) | (row >= 5)


def body(
    g_hbm, vel_hbm, vort_hbm, ta_hbm, tb_hbm, tc_hbm, tz_hbm, td_hbm, te_hbm,
    spec_out, grad_out,
    g, feat, ta, tb, tc, tz, td, te,
    data_a, send_a, recv_a, data_b, send_b, recv_b,
    lhs_c, work_c, lhs_z, work_z, send_c, recv_c, rhs, send_d, recv_d, lhs_e, spec,
    grad_acc, grad_part, grad_row, grad_sum_row, grad_col, grad_sum_col, grad_env,
    load_sem, ra_sem, rb_sem, rc_sem, rd_sem, sa_sem, sb_sem, sc_sem, sd_sem,
    grad_recv, grad_send, out_sem,
):
    env = lax.axis_index("env")
    row = lax.axis_index("row")
    col = lax.axis_index("col")
    col_active = is_active_col(col)
    row_active = is_active_row(row)

    def load_g(c):
        def one(kz, _):
            pltpu.make_async_copy(
                g_hbm.at[c, :, :, kz, :], g.at[c, kz], load_sem.at[1 + c]
            ).start()
            return 0

        lax.fori_loop(0, KZS, one, 0)

    half_a = pl.ds(0, 256)
    loads = [pltpu.make_async_copy(ta_hbm.at[half_a], ta.at[half_a], load_sem.at[0])]
    for c in range(3):
        loads.append(pltpu.make_async_copy(g.at[c], g.at[c], load_sem.at[1 + c]))
    loads.append(pltpu.make_async_copy(tb_hbm, tb, load_sem.at[4]))
    half_a = pl.ds(256, 256)
    loads.append(pltpu.make_async_copy(ta_hbm.at[half_a], ta.at[half_a], load_sem.at[11]))
    loads.append(pltpu.make_async_copy(tc_hbm, tc, load_sem.at[5]))
    loads.append(pltpu.make_async_copy(vel_hbm, feat.at[pl.ds(0, 3)], load_sem.at[6]))
    loads.append(pltpu.make_async_copy(vort_hbm, feat.at[pl.ds(3, 3)], load_sem.at[7]))
    loads.append(pltpu.make_async_copy(tz_hbm, tz, load_sem.at[8]))
    loads.append(pltpu.make_async_copy(td_hbm, td, load_sem.at[9]))
    loads.append(pltpu.make_async_copy(te_hbm, te, load_sem.at[10]))
    load_g(0)
    loads[0].start()
    barrier = pltpu.get_barrier_semaphore()

    def greet_row(k, _):
        pl.semaphore_signal(
            barrier, inc=1, device_id={"row": lax.rem(row + k, ROWS)}, device_id_type=MESH
        )
        return 0

    def greet_col(k, _):
        pl.semaphore_signal(
            barrier, inc=1, device_id={"col": lax.rem(col + k, COLS)}, device_id_type=MESH
        )
        return 0

    lax.fori_loop(1, ROWS, greet_row, 0)
    lax.fori_loop(1, COLS, greet_col, 0)
    pl.semaphore_signal(barrier, inc=1, device_id={"env": 1 - env}, device_id_type=MESH)

    load_g(1)
    loads[4].start()

    def start_row(c, j):
        def one(k, _):
            to = lax.rem(row + offset(k, ROWS), ROWS)
            pltpu.make_async_remote_copy(
                src_ref=send_a.at[c, j, to],
                dst_ref=recv_a.at[c, j, row],
                send_sem=sa_sem,
                recv_sem=ra_sem.at[c, j],
                device_id={"row": to},
                device_id_type=MESH,
            ).start()
            return 0

        lax.fori_loop(0, ROWS - 1, one, 0)
        pltpu.make_async_copy(send_a.at[c, j, row], recv_a.at[c, j, row], ra_sem.at[c, j]).start()

    def load_data(c):
        loads[1 + c].wait()
        for s in range(2):
            high, low = split(g[c, :, s].reshape(512, 256))
            data_a[:, 256 * s : 256 * s + 256] = high
            data_a[:, 512 + 256 * s : 768 + 256 * s] = high
            data_a[:, 1024 + 256 * s : 1280 + 256 * s] = low

    def stage_a(c, half):
        out = matmul_t(ta[256 * half : 256 * half + 256, :], data_a[...])
        for part in range(2):
            for t in range(2):
                for r in range(ROWS):
                    at = 128 * part + 64 * t + 8 * r
                    for m in range(4):
                        send_a[c, 2 * half + part, r, t, m] = out[
                            at : at + 8, 128 * m : 128 * m + 128
                        ]

    load_data(0)
    loads[0].wait()
    stage_a(0, 0)
    pl.semaphore_wait(barrier, ROWS - 1 + COLS - 1 + 1)
    start_row(0, 0)
    start_row(0, 1)
    loads[5].start()
    load_g(2)
    loads[5].wait()
    stage_a(0, 1)
    start_row(0, 2)
    start_row(0, 3)
    for load in loads[6:]:
        load.start()
    load_data(1)
    stage_a(1, 0)
    stage_a(1, 1)

    def sent(ref, sem):
        pltpu.make_async_copy(ref, ref, sem).wait()

    def sent_b(unit):
        sent(recv_b.at[0, pl.ds(0, COLS - 1), 0], sb_sem.at[unit])

    def sent_c(unit):
        @pl.when(col_active)
        def _():
            sent(send_c.at[0, 0, pl.ds(0, NCOL - 1)], sc_sem.at[unit])

        @pl.when(jnp.logical_not(col_active))
        def _():
            sent(send_c.at[0, 0], sc_sem.at[unit])

    def stage_b(unit, _):
        c = unit // PARTS
        j = unit % PARTS
        pltpu.make_async_copy(recv_a.at[c, j], recv_a.at[c, j], ra_sem.at[c, j]).wait()
        for t in range(2):
            for m in range(4):
                for group in range(2):
                    values = [recv_a[c, j, 4 * group + k, t, m] for k in range(4)]
                    values = exchange(values, 32)
                    at = 256 * t + 128 * group
                    for pair in range(2):
                        high, low = split(
                            jnp.concatenate((values[2 * pair], values[2 * pair + 1]), 0)
                        )
                        here = 32 * m + 16 * pair
                        data_b[here : here + 16, at : at + 128] = high
                        data_b[here : here + 16, at + 512 : at + 640] = high
                        data_b[here : here + 16, at + 1024 : at + 1152] = low
        out = matmul_t(tb[...], data_b[...])
        for t in range(2):
            send_b[c, j, t] = out[256 * t : 256 * t + 256, :]

        @pl.when(unit >= WINDOW_B)
        def _():
            sent_b(unit - WINDOW_B)

        def one(k, _):
            to = lax.rem(col + offset(k, COLS), COLS)
            pltpu.make_async_remote_copy(
                src_ref=send_b.at[c, j, :, pl.ds(KZS * to, KZS), :],
                dst_ref=recv_b.at[j, col, c],
                send_sem=sb_sem.at[unit],
                recv_sem=rb_sem.at[j],
                device_id={"col": to},
                device_id_type=MESH,
            ).start()
            return 0

        lax.fori_loop(0, COLS - 1, one, 0)
        pltpu.make_async_copy(
            send_b.at[c, j, :, pl.ds(KZS * col, KZS), :], recv_b.at[j, col, c], rb_sem.at[j]
        ).start()
        return 0

    loads[4].wait()
    stage_b(0, 0)
    for part in range(PARTS):
        start_row(1, part)
    stage_b(1, 0)
    load_data(2)
    stage_a(2, 0)
    stage_a(2, 1)
    for part in range(PARTS):
        start_row(2, part)
    lax.fori_loop(2, 3 * PARTS, stage_b, 0)

    for load in loads[6:]:
        load.wait()
    grad_acc[...] = jnp.zeros_like(grad_acc)

    def stage_d(unit, _):
        j = unit // 3
        c = unit % 3

        @pl.when(col_active)
        def _():
            pltpu.make_async_copy(recv_c.at[j, c], recv_c.at[j, c], rc_sem.at[j, c]).wait()
            for s in range(2):
                high, low = split(recv_c[j, c, s])
                rhs[256 * s : 256 * s + 256, :] = high
                rhs[512 + 256 * s : 768 + 256 * s, :] = high
                rhs[1024 + 256 * s : 1280 + 256 * s, :] = low
            out = matmul(td[...], rhs[...])
            for slot in range(NROW):
                for t in range(2):
                    at = 64 * slot + 32 * t
                    send_d[j, c, slot, t] = out[at : at + 32, :]

            mine = recv_d.at[j, c, row]

            def one(k, _):
                to = lax.rem(row + offset(k, ROWS), ROWS)

                @pl.when(is_active_row(to))
                def _():
                    pltpu.make_async_remote_copy(
                        src_ref=send_d.at[j, c, jnp.where(to < 3, to, to - 2)],
                        dst_ref=mine,
                        send_sem=sd_sem,
                        recv_sem=rd_sem.at[j, c],
                        device_id={"row": to},
                        device_id_type=MESH,
                    ).start()

                return 0

            lax.fori_loop(0, ROWS - 1, one, 0)

            @pl.when(row_active)
            def _():
                own = send_d.at[j, c, jnp.where(row < 3, row, row - 2)]
                pltpu.make_async_copy(own, mine, rd_sem.at[j, c]).start()

        return 0

    def stage_e(unit, _):
        j = unit // 3
        c = unit % 3

        @pl.when(col_active & row_active)
        def _():
            pltpu.make_async_copy(recv_d.at[j, c], recv_d.at[j, c], rd_sem.at[j, c]).wait()

            def gather(step, _):
                at = pl.multiple_of(16 * step, 16)
                values = [
                    recv_d[j, c, k & 7, k >> 3, pl.ds(at, 16), :] for k in range(16)
                ]
                values = exchange(values, 1)
                for kz in range(16):
                    high, low = split(values[kz])
                    rows = pl.ds(pl.multiple_of(KYS * kz + at, 16), 16)
                    lhs_e[rows, 0:128] = high
                    lhs_e[rows, 128:256] = high
                    lhs_e[rows, 256:384] = low
                return 0

            lax.fori_loop(0, 2, gather, 0)

            @pl.when(j == 0)
            def _():
                spec[c] = matmul(lhs_e[...], te[j])

            @pl.when(j > 0)
            def _():
                spec[c] += matmul(lhs_e[...], te[j])

            @pl.when(j == PARTS - 1)
            def _():
                def leave(kz, _):
                    rows = pl.ds(pl.multiple_of(KYS * kz, KYS), KYS)
                    pltpu.make_async_copy(
                        spec.at[c, rows], spec_out.at[c, :, kz, :], out_sem
                    ).start()
                    return 0

                lax.fori_loop(0, KZS, leave, 0)

        return 0

    def stage_c(j, _):
        pltpu.make_async_copy(recv_b.at[j], recv_b.at[j], rb_sem.at[j]).wait()

        def gather(step, _):
            c = step // 2
            s = step % 2
            for group in range(2):
                values = [recv_b[j, 8 * group + k, c, s] for k in range(8)]
                values = exchange(values, 1)
                at = pl.multiple_of(256 * s + 128 * group, 128)
                for x in range(8):
                    high, low = split(values[x])
                    rows = pl.ds(pl.multiple_of(128 * c + 16 * x, 16), 16)
                    lhs_c[rows, pl.ds(at, 128)] = high
                    lhs_c[rows, pl.ds(at + 512, 128)] = high
                    lhs_c[rows, pl.ds(at + 1024, 128)] = low
            return 0

        lax.fori_loop(0, 6, gather, 0)
        work_c[...] = matmul(lhs_c[...], tc[...])

        def cross(i, _):
            there = pl.ds(pl.multiple_of(128 * j + 16 * i, 16), 16)
            adjoint = [work_c[pl.ds(pl.multiple_of(128 * c + 16 * i, 16), 16), :] for c in range(3)]
            for f in range(6):
                feature = feat[f, there, :]
                for c in range(3):
                    product = adjoint[c] * feature
                    total = (product[:8, :128] + product[:8, 128:]) + (
                        product[8:, :128] + product[8:, 128:]
                    )
                    grad_acc[6 * c + f] += total
            spin = [feat[3 + c, there, :] for c in range(3)]
            for c in range(3):
                second, third = (c + 1) % 3, (c + 2) % 3
                high, low = split(
                    spin[second] * adjoint[third] - spin[third] * adjoint[second]
                )
                rows = pl.ds(pl.multiple_of(128 * c + 16 * i, 16), 16)
                lhs_z[rows, 0:256] = high
                lhs_z[rows, 256:512] = high
                lhs_z[rows, 512:768] = low
            return 0

        lax.fori_loop(0, 8, cross, 0)
        work_z[...] = matmul(lhs_z[...], tz[...])

        def scatter(c, _):
            for n in range(3):
                values = [
                    work_z[
                        pl.ds(pl.multiple_of(128 * c + 16 * x, 16), 16), 128 * n : 128 * n + 128
                    ]
                    for x in range(8)
                ]
                values = exchange(values, 16)
                for b in range(8):
                    block = 8 * n + b
                    send_c[j, c, block >> 1, block & 1] = values[b]

            unit = 3 * j + c

            @pl.when(unit >= WINDOW_C)
            def _():
                sent_c(unit - WINDOW_C)

            mine = recv_c.at[j, c, :, pl.ds(KZS * col, KZS), :]

            def one(k, _):
                to = lax.rem(col + offset(k, COLS), COLS)

                @pl.when(is_active_col(to))
                def _():
                    pltpu.make_async_remote_copy(
                        src_ref=send_c.at[j, c, jnp.where(to < 6, to, to - 4)],
                        dst_ref=mine,
                        send_sem=sc_sem.at[unit],
                        recv_sem=rc_sem.at[j, c],
                        device_id={"col": to},
                        device_id_type=MESH,
                    ).start()

                return 0

            lax.fori_loop(0, COLS - 1, one, 0)

            @pl.when(col_active)
            def _():
                own = send_c.at[j, c, jnp.where(col < 6, col, col - 4)]
                pltpu.make_async_copy(own, mine, rc_sem.at[j, c]).start()

            return 0

        lax.fori_loop(0, 3, scatter, 0)
        return 0

    stage_c(0, 0)
    stage_c(1, 0)
    lax.fori_loop(0, 3, stage_d, 0)
    stage_c(2, 0)
    lax.fori_loop(3, 6, stage_d, 0)
    lax.fori_loop(0, 3, stage_e, 0)
    stage_c(3, 0)

    for k in range(18):
        grad_part[k : k + 1, :] = jnp.sum(grad_acc[k], axis=0, keepdims=True)
    grad_part[18:24, :] = jnp.zeros((6, 128), F32)

    def share_row(k, _):
        pltpu.make_async_remote_copy(
            src_ref=grad_part,
            dst_ref=grad_row.at[row],
            send_sem=grad_send.at[0],
            recv_sem=grad_recv.at[0],
            device_id={"row": lax.rem(row + k, ROWS)},
            device_id_type=MESH,
        ).start()
        return 0

    lax.fori_loop(1, ROWS, share_row, 0)
    pltpu.make_async_copy(grad_part, grad_row.at[row], grad_recv.at[0]).start()

    sent(send_a.at[:, :, pl.ds(0, ROWS - 1)], sa_sem)
    for unit in range(3 * PARTS - WINDOW_B, 3 * PARTS):
        sent_b(unit)

    lax.fori_loop(6, 9, stage_d, 0)
    lax.fori_loop(3, 6, stage_e, 0)
    stage_d(9, 0)
    lax.fori_loop(6, 8, stage_e, 0)
    stage_d(10, 0)
    pltpu.make_async_copy(grad_row, grad_row, grad_recv.at[0]).wait()
    grad_sum_row[...] = jnp.sum(grad_row[...], axis=0)

    def share_col(k, _):
        pltpu.make_async_remote_copy(
            src_ref=grad_sum_row,
            dst_ref=grad_col.at[col],
            send_sem=grad_send.at[1],
            recv_sem=grad_recv.at[1],
            device_id={"col": lax.rem(col + k, COLS)},
            device_id_type=MESH,
        ).start()
        return 0

    lax.fori_loop(1, COLS, share_col, 0)
    pltpu.make_async_copy(grad_sum_row, grad_col.at[col], grad_recv.at[1]).start()

    stage_e(8, 0)
    stage_d(11, 0)
    pltpu.make_async_copy(grad_col, grad_col, grad_recv.at[1]).wait()
    grad_sum_col[...] = jnp.sum(grad_col[...], axis=0)
    pltpu.make_async_remote_copy(
        src_ref=grad_sum_col,
        dst_ref=grad_env.at[env],
        send_sem=grad_send.at[2],
        recv_sem=grad_recv.at[2],
        device_id={"env": 1 - env},
        device_id_type=MESH,
    ).start()
    pltpu.make_async_copy(grad_sum_col, grad_env.at[env], grad_recv.at[2]).start()

    stage_e(9, 0)
    stage_e(10, 0)
    pltpu.make_async_copy(grad_env, grad_env, grad_recv.at[2]).wait()
    total = jnp.sum(grad_env[0] + grad_env[1], axis=1, keepdims=True)
    total = total * (1.0 / math.sqrt(2 * N**3))
    lane = lax.broadcasted_iota(jnp.int32, (1, 6), 1)
    for c in range(3):
        line = jnp.zeros((1, 6), F32)
        for f in range(6):
            line = jnp.where(lane == f, total[6 * c + f : 6 * c + f + 1, :], line)
        grad_out[c : c + 1, :] = line

    for unit in range(3 * PARTS - WINDOW_C, 3 * PARTS):
        sent_c(unit)
    sent(grad_row.at[pl.ds(0, ROWS - 1)], grad_send.at[0])
    sent(grad_col.at[pl.ds(0, COLS - 1)], grad_send.at[1])
    sent(grad_env.at[0], grad_send.at[2])

    stage_e(11, 0)

    @pl.when(col_active)
    def _():
        @pl.when(row_active)
        def _():
            sent(send_d.at[:, :, pl.ds(0, NROW - 1)], sd_sem)
            sent(spec, out_sem)

        @pl.when(jnp.logical_not(row_active))
        def _():
            sent(send_d, sd_sem)


def last_body(spec, sums, out, grad, before, after, in_sem, out_sem):
    row = lax.axis_index("row")
    col = lax.axis_index("col")
    active = is_active_col(col) & is_active_row(row)
    grad[...] = sums[...]

    lines = KYS // TILES

    def leave(tile, source):
        pltpu.make_async_copy(
            after.at[source], out.at[:, :, pl.ds(lines * tile, lines)], out_sem
        ).start()

    @pl.when(jnp.logical_not(active))
    def _():
        after[0] = jnp.zeros(after.shape[1:], F32)

        def one(tile, _):
            leave(tile, 0)
            return 0

        lax.fori_loop(0, TILES, one, 0)

    @pl.when(active)
    def _():
        def enter(tile, _):
            pltpu.make_async_copy(
                spec.at[:, pl.ds(lines * tile, lines)], before.at[tile], in_sem.at[tile]
            ).start()
            return 0

        lax.fori_loop(0, TILES, enter, 0)

        def signed(index):
            return jnp.where(index < N // 2, index, index - N).astype(F32)

        wave_x = signed(lax.broadcasted_iota(jnp.int32, (8, 256), 1))
        down = lax.broadcasted_iota(jnp.int32, (8, 256), 0)

        def project(tile, _):
            pltpu.make_async_copy(before.at[tile], before.at[tile], in_sem.at[tile]).wait()
            for line in range(lines):
                wave_y = signed(jnp.full((8, 256), KYS * row + lines * tile + line, jnp.int32))
                for part in range(2):
                    wave_z = signed(down + (KZS * col + 8 * part))
                    kept = (
                        (3.0 * jnp.abs(wave_x) < N)
                        & (3.0 * jnp.abs(wave_y) < N)
                        & (3.0 * jnp.abs(wave_z) < N)
                    )
                    square = wave_x * wave_x + wave_y * wave_y + wave_z * wave_z
                    inverse = 1.0 / jnp.maximum(square, 1.0)
                    waves = (wave_x, wave_y, wave_z)
                    here = slice(8 * part, 8 * part + 8)
                    for t in range(2):
                        parts = [
                            before[tile, c, line, here, 256 * t : 256 * t + 256]
                            for c in range(3)
                        ]
                        inner = (
                            wave_x * parts[0] + wave_y * parts[1] + wave_z * parts[2]
                        ) * inverse
                        for c in range(3):
                            after[tile, c, t, line, here, :] = jnp.where(
                                kept, parts[c] - waves[c] * inner, 0.0
                            )
            leave(tile, tile)
            return 0

        lax.fori_loop(0, TILES, project, 0)

    pltpu.make_async_copy(after, after, out_sem).wait()


def shards(adjoint_hat, velocity, vorticity):
    constants = [jnp.asarray(t) for t in tables()]
    hbm = pl.BlockSpec(memory_space=pl.ANY)
    vmem = pltpu.VMEM
    dma = pltpu.SemaphoreType.DMA
    spec, grad = pl.pallas_call(
        body,
        name="advect",
        out_shape=(
            jax.ShapeDtypeStruct((3, KYS, KZS, 512), F32),
            jax.ShapeDtypeStruct((3, 6), F32),
        ),
        in_specs=[hbm] * 9,
        out_specs=(hbm, pl.BlockSpec(memory_space=pltpu.VMEM)),
        scratch_shapes=[
            vmem((3, KZS, 2, KYS, 256), F32),
            vmem((6, 512, 256), F32),
            vmem((512, 1536), BF16),
            vmem((512, 1536), BF16),
            vmem((1536, 256), BF16),
            vmem((768, 384), BF16),
            vmem((384, 1536), BF16),
            vmem((PARTS, 384, 512), BF16),
            vmem((512, 1536), BF16),
            vmem((3, PARTS, ROWS, 2, 4, 8, 128), F32),
            vmem((3, PARTS, ROWS, 2, 4, 8, 128), F32),
            vmem((128, 1536), BF16),
            vmem((3, PARTS, 2, N, 128), F32),
            vmem((PARTS, COLS, 3, 2, KZS, 128), F32),
            vmem((384, 1536), BF16),
            vmem((384, 256), F32),
            vmem((384, 768), BF16),
            vmem((384, 384), F32),
            vmem((PARTS, 3, NCOL, 2, KZS, 128), F32),
            vmem((PARTS, 3, 2, N, 128), F32),
            vmem((1536, 128), BF16),
            vmem((PARTS, 3, NROW, 2, KYS, 128), F32),
            vmem((PARTS, 3, ROWS, 2, KYS, 128), F32),
            vmem((512, 384), BF16),
            vmem((3, 512, 512), F32),
            vmem((18, 8, 128), F32),
            vmem((24, 128), F32),
            vmem((ROWS, 24, 128), F32),
            vmem((24, 128), F32),
            vmem((COLS, 24, 128), F32),
            vmem((24, 128), F32),
            vmem((2, 24, 128), F32),
            dma((12,)),
            dma((3, PARTS)),
            dma((PARTS,)),
            dma((PARTS, 3)),
            dma((PARTS, 3)),
            dma,
            dma((3 * PARTS,)),
            dma((3 * PARTS,)),
            dma,
            dma((3,)),
            dma((3,)),
            dma,
        ],
        compiler_params=pltpu.CompilerParams(
            collective_id=0, has_side_effects=True, vmem_limit_bytes=60 * 2**20
        ),
    )(
        adjoint_hat[0],
        velocity.reshape(3, 512, 256),
        vorticity.reshape(3, 512, 256),
        *constants,
    )
    out, grad = pl.pallas_call(
        last_body,
        name="project",
        out_shape=(
            jax.ShapeDtypeStruct((3, 2, KYS, KZS, N), F32),
            jax.ShapeDtypeStruct((3, 6), F32),
        ),
        in_specs=[hbm, pl.BlockSpec(memory_space=pltpu.VMEM)],
        out_specs=(hbm, pl.BlockSpec(memory_space=pltpu.VMEM)),
        scratch_shapes=[
            vmem((TILES, 3, KYS // TILES, KZS, 512), F32),
            vmem((TILES, 3, 2, KYS // TILES, KZS, N), F32),
            dma((TILES,)),
            dma,
        ],
        compiler_params=pltpu.CompilerParams(vmem_limit_bytes=60 * 2**20),
    )(spec, grad)
    return out.reshape(adjoint_hat.shape), grad


def solution(mesh):
    placed = (
        P("env", None, None, "row", "col", None),
        P("env", None, "row", "col", None),
        P("env", None, "row", "col", None),
    )
    return jax.shard_map(
        shards,
        mesh=mesh,
        in_specs=placed,
        out_specs=(P("env", None, None, "row", "col", None), P()),
        check_vma=False,
    )
```

```python
import math

import jax
import jax.numpy as jnp
import ml_dtypes
import numpy as np
from jax import lax
from jax.experimental import pallas as pl
from jax.experimental.pallas import tpu as pltpu
from jax.sharding import PartitionSpec as P

F32 = jnp.float32
BF16 = jnp.bfloat16
MESH = pl.DeviceIdType.MESH

N = 256
ROWS = 8
COLS = 16
KYS = 32
KZS = 16
PARTS = 4
WINDOW_B = 2
WINDOW_C = 2
ACTIVE_COLS = (0, 1, 2, 3, 4, 5, 10, 11, 12, 13, 14, 15)
ACTIVE_ROWS = (0, 1, 2, 5, 6, 7)
NCOL = len(ACTIVE_COLS)
NROW = len(ACTIVE_ROWS)


def halves(table):
    high = table.astype(np.float32).astype(ml_dtypes.bfloat16)
    low = (table - high.astype(np.float64)).astype(np.float32).astype(ml_dtypes.bfloat16)
    return high, low


def stacked(table, axis):
    high, low = halves(table)
    return np.concatenate((high, low, high), axis)


def wave(out_index, in_index):
    angles = (np.outer(out_index, in_index) % N) * (2.0 * math.pi / N)
    return np.cos(angles) / math.sqrt(N), np.sin(angles) / math.sqrt(N)


def x_order():
    order = np.zeros((PARTS, ROWS, 8), np.int64)
    for part in range(PARTS):
        for row in range(ROWS):
            order[part, row] = 32 * row + 8 * part + np.arange(8)
    return order


def tables():
    every = np.arange(N)
    order = x_order()
    pieces = []
    for part in range(PARTS):
        cosines, sines = wave(order[part].reshape(-1), every)
        pieces.append(np.block([[cosines, -sines], [sines, cosines]]))
    table_a = stacked(np.concatenate(pieces, 0), 1)
    cosines, sines = wave(every, every)
    table_b = stacked(np.block([[cosines, -sines], [sines, cosines]]), 1)
    kz_order = np.arange(N).reshape(2, 8, KZS).transpose(0, 2, 1).reshape(-1)
    table_c = stacked(np.concatenate((cosines[kz_order], -sines[kz_order]), 0), 0)
    pieces = []
    for col in ACTIVE_COLS:
        kept = slice(KZS * col, KZS * col + KZS)
        pieces += [cosines[:, kept], -sines[:, kept]]
    table_z = stacked(np.concatenate(pieces, 1), 0)
    pieces = []
    for row in ACTIVE_ROWS:
        kept = slice(KYS * row, KYS * row + KYS)
        pieces.append(np.concatenate((cosines[kept], sines[kept]), 1))
        pieces.append(np.concatenate((-sines[kept], cosines[kept]), 1))
    table_d = stacked(np.concatenate(pieces, 0), 1)
    table_e = []
    for part in range(PARTS):
        block = np.zeros((8, 2, ROWS, 2, N))
        for row in range(ROWS):
            cosines, sines = wave(order[part, row], every)
            block[:, 0, row, 0], block[:, 0, row, 1] = cosines, -sines
            block[:, 1, row, 0], block[:, 1, row, 1] = sines, cosines
        table_e.append(stacked(block.reshape(128, 2 * N), 0))
    return table_a, table_b, table_c, table_z, table_d, np.stack(table_e)


def exchange(values, lane_bits):
    values = list(values)
    lane = lax.broadcasted_iota(jnp.int32, values[0].shape, 1)
    bit = 1
    while bit < len(values):
        step = bit * lane_bits
        clear = (lane & step) == 0
        for low in range(len(values)):
            if low & bit:
                continue
            first, second = values[low], values[low | bit]
            values[low] = jnp.where(clear, first, pltpu.roll(second, step, 1))
            values[low | bit] = jnp.where(clear, pltpu.roll(first, 128 - step, 1), second)
        bit *= 2
    return values


def split(value):
    high = value.astype(BF16)
    low = (value - high.astype(F32)).astype(BF16)
    return high, low


def matmul(left, right):
    return jnp.dot(left, right, preferred_element_type=F32)


def matmul_t(left, right):
    return lax.dot_general(
        left, right, (((1,), (1,)), ((), ())), preferred_element_type=F32
    )


def offset(k, size):
    step = k
    away = step // 2 + 1
    return jnp.where(step % 2 == 0, away, size - away)


def is_active_col(col):
    return (col < 6) | (col >= 10)


def is_active_row(row):
    return (row < 3) | (row >= 5)


def body(
    g_hbm, vel_hbm, vort_hbm, ta_hbm, tb_hbm, tc_hbm, tz_hbm, td_hbm, te_hbm,
    spec_out, grad_out,
    g, feat, ta, tb, tc, tz, td, te,
    data_a, send_a, recv_a, data_b, send_b, recv_b,
    lhs_c, work_c, lhs_z, work_z, send_c, recv_c, rhs, send_d, recv_d, lhs_e, spec,
    grad_acc, grad_part, grad_row, grad_sum_row, grad_col, grad_sum_col, grad_env,
    load_sem, ra_sem, rb_sem, rc_sem, rd_sem, sa_sem, sb_sem, sc_sem, sd_sem,
    grad_recv, grad_send, out_sem,
):
    env = lax.axis_index("env")
    row = lax.axis_index("row")
    col = lax.axis_index("col")
    col_active = is_active_col(col)
    row_active = is_active_row(row)

    def load_g(c):
        def one(kz, _):
            pltpu.make_async_copy(
                g_hbm.at[c, :, :, kz, :], g.at[c, kz], load_sem.at[1 + c]
            ).start()
            return 0

        lax.fori_loop(0, KZS, one, 0)

    half_a = pl.ds(0, 256)
    loads = [pltpu.make_async_copy(ta_hbm.at[half_a], ta.at[half_a], load_sem.at[0])]
    for c in range(3):
        loads.append(pltpu.make_async_copy(g.at[c], g.at[c], load_sem.at[1 + c]))
    loads.append(pltpu.make_async_copy(tb_hbm, tb, load_sem.at[4]))
    half_a = pl.ds(256, 256)
    loads.append(pltpu.make_async_copy(ta_hbm.at[half_a], ta.at[half_a], load_sem.at[11]))
    loads.append(pltpu.make_async_copy(tc_hbm, tc, load_sem.at[5]))
    loads.append(pltpu.make_async_copy(vel_hbm, feat.at[pl.ds(0, 3)], load_sem.at[6]))
    loads.append(pltpu.make_async_copy(vort_hbm, feat.at[pl.ds(3, 3)], load_sem.at[7]))
    loads.append(pltpu.make_async_copy(tz_hbm, tz, load_sem.at[8]))
    loads.append(pltpu.make_async_copy(td_hbm, td, load_sem.at[9]))
    loads.append(pltpu.make_async_copy(te_hbm, te, load_sem.at[10]))
    load_g(0)
    loads[0].start()
    barrier = pltpu.get_barrier_semaphore()

    def greet_row(k, _):
        pl.semaphore_signal(
            barrier, inc=1, device_id={"row": lax.rem(row + k, ROWS)}, device_id_type=MESH
        )
        return 0

    def greet_col(k, _):
        pl.semaphore_signal(
            barrier, inc=1, device_id={"col": lax.rem(col + k, COLS)}, device_id_type=MESH
        )
        return 0

    lax.fori_loop(1, ROWS, greet_row, 0)
    lax.fori_loop(1, COLS, greet_col, 0)
    pl.semaphore_signal(barrier, inc=1, device_id={"env": 1 - env}, device_id_type=MESH)

    load_g(1)
    loads[4].start()

    def start_row(c, j):
        def one(k, _):
            to = lax.rem(row + offset(k, ROWS), ROWS)
            pltpu.make_async_remote_copy(
                src_ref=send_a.at[c, j, to],
                dst_ref=recv_a.at[c, j, row],
                send_sem=sa_sem,
                recv_sem=ra_sem.at[c, j],
                device_id={"row": to},
                device_id_type=MESH,
            ).start()
            return 0

        lax.fori_loop(0, ROWS - 1, one, 0)
        pltpu.make_async_copy(send_a.at[c, j, row], recv_a.at[c, j, row], ra_sem.at[c, j]).start()

    def load_data(c):
        loads[1 + c].wait()
        for s in range(2):
            high, low = split(g[c, :, s].reshape(512, 256))
            data_a[:, 256 * s : 256 * s + 256] = high
            data_a[:, 512 + 256 * s : 768 + 256 * s] = high
            data_a[:, 1024 + 256 * s : 1280 + 256 * s] = low

    def stage_a(c, half):
        out = matmul_t(ta[256 * half : 256 * half + 256, :], data_a[...])
        for part in range(2):
            for t in range(2):
                for r in range(ROWS):
                    at = 128 * part + 64 * t + 8 * r
                    for m in range(4):
                        send_a[c, 2 * half + part, r, t, m] = out[
                            at : at + 8, 128 * m : 128 * m + 128
                        ]

    load_data(0)
    loads[0].wait()
    stage_a(0, 0)
    pl.semaphore_wait(barrier, ROWS - 1 + COLS - 1 + 1)
    start_row(0, 0)
    start_row(0, 1)
    loads[5].start()
    load_g(2)
    loads[5].wait()
    stage_a(0, 1)
    start_row(0, 2)
    start_row(0, 3)
    for load in loads[6:]:
        load.start()
    load_data(1)
    stage_a(1, 0)
    stage_a(1, 1)

    def sent(ref, sem):
        pltpu.make_async_copy(ref, ref, sem).wait()

    def sent_b(unit):
        sent(recv_b.at[0, pl.ds(0, COLS - 1), 0], sb_sem.at[unit])

    def sent_c(unit):
        @pl.when(col_active)
        def _():
            sent(send_c.at[0, 0, pl.ds(0, NCOL - 1)], sc_sem.at[unit])

        @pl.when(jnp.logical_not(col_active))
        def _():
            sent(send_c.at[0, 0], sc_sem.at[unit])

    def stage_b(unit, _):
        c = unit // PARTS
        j = unit % PARTS
        pltpu.make_async_copy(recv_a.at[c, j], recv_a.at[c, j], ra_sem.at[c, j]).wait()
        for t in range(2):
            for m in range(4):
                for group in range(2):
                    values = [recv_a[c, j, 4 * group + k, t, m] for k in range(4)]
                    values = exchange(values, 32)
                    at = 256 * t + 128 * group
                    for pair in range(2):
                        high, low = split(
                            jnp.concatenate((values[2 * pair], values[2 * pair + 1]), 0)
                        )
                        here = 32 * m + 16 * pair
                        data_b[here : here + 16, at : at + 128] = high
                        data_b[here : here + 16, at + 512 : at + 640] = high
                        data_b[here : here + 16, at + 1024 : at + 1152] = low
        out = matmul_t(tb[...], data_b[...])
        for t in range(2):
            send_b[c, j, t] = out[256 * t : 256 * t + 256, :]

        @pl.when(unit >= WINDOW_B)
        def _():
            sent_b(unit - WINDOW_B)

        def one(k, _):
            to = lax.rem(col + offset(k, COLS), COLS)
            pltpu.make_async_remote_copy(
                src_ref=send_b.at[c, j, :, pl.ds(KZS * to, KZS), :],
                dst_ref=recv_b.at[j, col, c],
                send_sem=sb_sem.at[unit],
                recv_sem=rb_sem.at[j],
                device_id={"col": to},
                device_id_type=MESH,
            ).start()
            return 0

        lax.fori_loop(0, COLS - 1, one, 0)
        pltpu.make_async_copy(
            send_b.at[c, j, :, pl.ds(KZS * col, KZS), :], recv_b.at[j, col, c], rb_sem.at[j]
        ).start()
        return 0

    loads[4].wait()
    stage_b(0, 0)
    for part in range(PARTS):
        start_row(1, part)
    stage_b(1, 0)
    load_data(2)
    stage_a(2, 0)
    stage_a(2, 1)
    for part in range(PARTS):
        start_row(2, part)
    lax.fori_loop(2, 3 * PARTS, stage_b, 0)

    for load in loads[6:]:
        load.wait()
    grad_acc[...] = jnp.zeros_like(grad_acc)

    def stage_d(unit, _):
        j = unit // 3
        c = unit % 3

        @pl.when(col_active)
        def _():
            pltpu.make_async_copy(recv_c.at[j, c], recv_c.at[j, c], rc_sem.at[j, c]).wait()
            for s in range(2):
                high, low = split(recv_c[j, c, s])
                rhs[256 * s : 256 * s + 256, :] = high
                rhs[512 + 256 * s : 768 + 256 * s, :] = high
                rhs[1024 + 256 * s : 1280 + 256 * s, :] = low
            out = matmul(td[...], rhs[...])
            for slot in range(NROW):
                for t in range(2):
                    at = 64 * slot + 32 * t
                    send_d[j, c, slot, t] = out[at : at + 32, :]

            mine = recv_d.at[j, c, row]

            def one(k, _):
                to = lax.rem(row + offset(k, ROWS), ROWS)

                @pl.when(is_active_row(to))
                def _():
                    pltpu.make_async_remote_copy(
                        src_ref=send_d.at[j, c, jnp.where(to < 3, to, to - 2)],
                        dst_ref=mine,
                        send_sem=sd_sem,
                        recv_sem=rd_sem.at[j, c],
                        device_id={"row": to},
                        device_id_type=MESH,
                    ).start()

                return 0

            lax.fori_loop(0, ROWS - 1, one, 0)

            @pl.when(row_active)
            def _():
                own = send_d.at[j, c, jnp.where(row < 3, row, row - 2)]
                pltpu.make_async_copy(own, mine, rd_sem.at[j, c]).start()

        return 0

    def stage_e(unit, _):
        j = unit // 3
        c = unit % 3

        @pl.when(col_active & row_active)
        def _():
            pltpu.make_async_copy(recv_d.at[j, c], recv_d.at[j, c], rd_sem.at[j, c]).wait()

            def gather(step, _):
                at = pl.multiple_of(16 * step, 16)
                values = [
                    recv_d[j, c, k & 7, k >> 3, pl.ds(at, 16), :] for k in range(16)
                ]
                values = exchange(values, 1)
                for kz in range(16):
                    high, low = split(values[kz])
                    rows = pl.ds(pl.multiple_of(KYS * kz + at, 16), 16)
                    lhs_e[rows, 0:128] = high
                    lhs_e[rows, 128:256] = high
                    lhs_e[rows, 256:384] = low
                return 0

            lax.fori_loop(0, 2, gather, 0)

            @pl.when(j == 0)
            def _():
                spec[c] = matmul(lhs_e[...], te[j])

            @pl.when(j > 0)
            def _():
                spec[c] += matmul(lhs_e[...], te[j])

            @pl.when(j == PARTS - 1)
            def _():
                pltpu.make_async_copy(spec.at[c], spec_out.at[c], out_sem).start()

        return 0

    def stage_c(j, _):
        pltpu.make_async_copy(recv_b.at[j], recv_b.at[j], rb_sem.at[j]).wait()

        def gather(step, _):
            c = step // 2
            s = step % 2
            for group in range(2):
                values = [recv_b[j, 8 * group + k, c, s] for k in range(8)]
                values = exchange(values, 1)
                at = pl.multiple_of(256 * s + 128 * group, 128)
                for x in range(8):
                    high, low = split(values[x])
                    rows = pl.ds(pl.multiple_of(128 * c + 16 * x, 16), 16)
                    lhs_c[rows, pl.ds(at, 128)] = high
                    lhs_c[rows, pl.ds(at + 512, 128)] = high
                    lhs_c[rows, pl.ds(at + 1024, 128)] = low
            return 0

        lax.fori_loop(0, 6, gather, 0)
        work_c[...] = matmul(lhs_c[...], tc[...])

        def cross(i, _):
            there = pl.ds(pl.multiple_of(128 * j + 16 * i, 16), 16)
            adjoint = [work_c[pl.ds(pl.multiple_of(128 * c + 16 * i, 16), 16), :] for c in range(3)]
            for f in range(6):
                feature = feat[f, there, :]
                for c in range(3):
                    product = adjoint[c] * feature
                    total = (product[:8, :128] + product[:8, 128:]) + (
                        product[8:, :128] + product[8:, 128:]
                    )
                    grad_acc[6 * c + f] += total
            spin = [feat[3 + c, there, :] for c in range(3)]
            for c in range(3):
                second, third = (c + 1) % 3, (c + 2) % 3
                high, low = split(
                    spin[second] * adjoint[third] - spin[third] * adjoint[second]
                )
                rows = pl.ds(pl.multiple_of(128 * c + 16 * i, 16), 16)
                lhs_z[rows, 0:256] = high
                lhs_z[rows, 256:512] = high
                lhs_z[rows, 512:768] = low
            return 0

        lax.fori_loop(0, 8, cross, 0)
        work_z[...] = matmul(lhs_z[...], tz[...])

        def scatter(c, _):
            for n in range(3):
                values = [
                    work_z[
                        pl.ds(pl.multiple_of(128 * c + 16 * x, 16), 16), 128 * n : 128 * n + 128
                    ]
                    for x in range(8)
                ]
                values = exchange(values, 16)
                for b in range(8):
                    block = 8 * n + b
                    send_c[j, c, block >> 1, block & 1] = values[b]

            unit = 3 * j + c

            @pl.when(unit >= WINDOW_C)
            def _():
                sent_c(unit - WINDOW_C)

            mine = recv_c.at[j, c, :, pl.ds(KZS * col, KZS), :]

            def one(k, _):
                to = lax.rem(col + offset(lax.rem(k, COLS - 1), COLS), COLS)

                @pl.when(jnp.where(k < COLS - 1, to < 6, to >= 10))
                def _():
                    pltpu.make_async_remote_copy(
                        src_ref=send_c.at[j, c, jnp.where(to < 6, to, to - 4)],
                        dst_ref=mine,
                        send_sem=sc_sem.at[unit],
                        recv_sem=rc_sem.at[j, c],
                        device_id={"col": to},
                        device_id_type=MESH,
                    ).start()

                return 0

            lax.fori_loop(0, 2 * (COLS - 1), one, 0)

            @pl.when(col_active)
            def _():
                own = send_c.at[j, c, jnp.where(col < 6, col, col - 4)]
                pltpu.make_async_copy(own, mine, rc_sem.at[j, c]).start()

            return 0

        lax.fori_loop(0, 3, scatter, 0)
        return 0

    stage_c(0, 0)
    stage_c(1, 0)
    lax.fori_loop(0, 3, stage_d, 0)
    stage_c(2, 0)
    lax.fori_loop(3, 6, stage_d, 0)
    lax.fori_loop(0, 3, stage_e, 0)
    stage_c(3, 0)

    for k in range(18):
        grad_part[k : k + 1, :] = jnp.sum(grad_acc[k], axis=0, keepdims=True)
    grad_part[18:24, :] = jnp.zeros((6, 128), F32)

    def share_row(k, _):
        pltpu.make_async_remote_copy(
            src_ref=grad_part,
            dst_ref=grad_row.at[row],
            send_sem=grad_send.at[0],
            recv_sem=grad_recv.at[0],
            device_id={"row": lax.rem(row + k, ROWS)},
            device_id_type=MESH,
        ).start()
        return 0

    lax.fori_loop(1, ROWS, share_row, 0)
    pltpu.make_async_copy(grad_part, grad_row.at[row], grad_recv.at[0]).start()

    sent(send_a.at[:, :, pl.ds(0, ROWS - 1)], sa_sem)
    for unit in range(3 * PARTS - WINDOW_B, 3 * PARTS):
        sent_b(unit)

    lax.fori_loop(6, 9, stage_d, 0)
    lax.fori_loop(3, 6, stage_e, 0)
    stage_d(9, 0)
    lax.fori_loop(6, 8, stage_e, 0)
    stage_d(10, 0)
    pltpu.make_async_copy(grad_row, grad_row, grad_recv.at[0]).wait()
    grad_sum_row[...] = jnp.sum(grad_row[...], axis=0)

    def share_col(k, _):
        pltpu.make_async_remote_copy(
            src_ref=grad_sum_row,
            dst_ref=grad_col.at[col],
            send_sem=grad_send.at[1],
            recv_sem=grad_recv.at[1],
            device_id={"col": lax.rem(col + k, COLS)},
            device_id_type=MESH,
        ).start()
        return 0

    lax.fori_loop(1, COLS, share_col, 0)
    pltpu.make_async_copy(grad_sum_row, grad_col.at[col], grad_recv.at[1]).start()

    stage_e(8, 0)
    stage_d(11, 0)
    pltpu.make_async_copy(grad_col, grad_col, grad_recv.at[1]).wait()
    grad_sum_col[...] = jnp.sum(grad_col[...], axis=0)
    pltpu.make_async_remote_copy(
        src_ref=grad_sum_col,
        dst_ref=grad_env.at[env],
        send_sem=grad_send.at[2],
        recv_sem=grad_recv.at[2],
        device_id={"env": 1 - env},
        device_id_type=MESH,
    ).start()
    pltpu.make_async_copy(grad_sum_col, grad_env.at[env], grad_recv.at[2]).start()

    stage_e(9, 0)
    stage_e(10, 0)
    pltpu.make_async_copy(grad_env, grad_env, grad_recv.at[2]).wait()
    total = jnp.sum(grad_env[0] + grad_env[1], axis=1, keepdims=True)
    total = total * (1.0 / math.sqrt(2 * N**3))
    lane = lax.broadcasted_iota(jnp.int32, (1, 6), 1)
    for c in range(3):
        line = jnp.zeros((1, 6), F32)
        for f in range(6):
            line = jnp.where(lane == f, total[6 * c + f : 6 * c + f + 1, :], line)
        grad_out[c : c + 1, :] = line

    for unit in range(3 * PARTS - WINDOW_C, 3 * PARTS):
        sent_c(unit)
    sent(grad_row.at[pl.ds(0, ROWS - 1)], grad_send.at[0])
    sent(grad_col.at[pl.ds(0, COLS - 1)], grad_send.at[1])
    sent(grad_env.at[0], grad_send.at[2])

    stage_e(11, 0)

    @pl.when(col_active)
    def _():
        @pl.when(row_active)
        def _():
            sent(send_d.at[:, :, pl.ds(0, NROW - 1)], sd_sem)
            sent(spec, out_sem)

        @pl.when(jnp.logical_not(row_active))
        def _():
            sent(send_d, sd_sem)


def last_body(spec, sums, out, grad, before, after, in_sem, out_sem):
    row = lax.axis_index("row")
    col = lax.axis_index("col")
    active = is_active_col(col) & is_active_row(row)
    grad[...] = sums[...]

    def leave(kz, source):
        pltpu.make_async_copy(after.at[source], out.at[:, :, :, kz, :], out_sem).start()

    @pl.when(jnp.logical_not(active))
    def _():
        after[0] = jnp.zeros(after.shape[1:], F32)

        def one(kz, _):
            leave(kz, 0)
            return 0

        lax.fori_loop(0, KZS, one, 0)

    @pl.when(active)
    def _():
        def enter(kz, _):
            pltpu.make_async_copy(spec.at[:, kz], before.at[kz], in_sem.at[kz]).start()
            return 0

        lax.fori_loop(0, KZS, enter, 0)

        def signed(index):
            return jnp.where(index < N // 2, index, index - N).astype(F32)

        wave_x = signed(lax.broadcasted_iota(jnp.int32, (8, 256), 1))
        lines = lax.broadcasted_iota(jnp.int32, (8, 256), 0)

        def project(kz, _):
            pltpu.make_async_copy(before.at[kz], before.at[kz], in_sem.at[kz]).wait()
            wave_z = signed(jnp.full((8, 256), KZS * col + kz, jnp.int32))
            for tile in range(4):
                wave_y = signed(lines + (KYS * row + 8 * tile))
                kept = (
                    (3.0 * jnp.abs(wave_x) < N)
                    & (3.0 * jnp.abs(wave_y) < N)
                    & (3.0 * jnp.abs(wave_z) < N)
                )
                square = wave_x * wave_x + wave_y * wave_y + wave_z * wave_z
                inverse = 1.0 / jnp.maximum(square, 1.0)
                waves = (wave_x, wave_y, wave_z)
                here = slice(8 * tile, 8 * tile + 8)
                for t in range(2):
                    parts = [
                        before[kz, c, here, 256 * t : 256 * t + 256] for c in range(3)
                    ]
                    inner = (
                        wave_x * parts[0] + wave_y * parts[1] + wave_z * parts[2]
                    ) * inverse
                    for c in range(3):
                        after[kz, c, t, here, :] = jnp.where(
                            kept, parts[c] - waves[c] * inner, 0.0
                        )
            leave(kz, kz)
            return 0

        lax.fori_loop(0, KZS, project, 0)

    pltpu.make_async_copy(after, after, out_sem).wait()


def shards(adjoint_hat, velocity, vorticity):
    constants = [jnp.asarray(t) for t in tables()]
    hbm = pl.BlockSpec(memory_space=pl.ANY)
    vmem = pltpu.VMEM
    dma = pltpu.SemaphoreType.DMA
    spec, grad = pl.pallas_call(
        body,
        name="advect",
        out_shape=(
            jax.ShapeDtypeStruct((3, 512, 512), F32),
            jax.ShapeDtypeStruct((3, 6), F32),
        ),
        in_specs=[hbm] * 9,
        out_specs=(hbm, pl.BlockSpec(memory_space=pltpu.VMEM)),
        scratch_shapes=[
            vmem((3, KZS, 2, KYS, 256), F32),
            vmem((6, 512, 256), F32),
            vmem((512, 1536), BF16),
            vmem((512, 1536), BF16),
            vmem((1536, 256), BF16),
            vmem((768, 384), BF16),
            vmem((384, 1536), BF16),
            vmem((PARTS, 384, 512), BF16),
            vmem((512, 1536), BF16),
            vmem((3, PARTS, ROWS, 2, 4, 8, 128), F32),
            vmem((3, PARTS, ROWS, 2, 4, 8, 128), F32),
            vmem((128, 1536), BF16),
            vmem((3, PARTS, 2, N, 128), F32),
            vmem((PARTS, COLS, 3, 2, KZS, 128), F32),
            vmem((384, 1536), BF16),
            vmem((384, 256), F32),
            vmem((384, 768), BF16),
            vmem((384, 384), F32),
            vmem((PARTS, 3, NCOL, 2, KZS, 128), F32),
            vmem((PARTS, 3, 2, N, 128), F32),
            vmem((1536, 128), BF16),
            vmem((PARTS, 3, NROW, 2, KYS, 128), F32),
            vmem((PARTS, 3, ROWS, 2, KYS, 128), F32),
            vmem((512, 384), BF16),
            vmem((3, 512, 512), F32),
            vmem((18, 8, 128), F32),
            vmem((24, 128), F32),
            vmem((ROWS, 24, 128), F32),
            vmem((24, 128), F32),
            vmem((COLS, 24, 128), F32),
            vmem((24, 128), F32),
            vmem((2, 24, 128), F32),
            dma((12,)),
            dma((3, PARTS)),
            dma((PARTS,)),
            dma((PARTS, 3)),
            dma((PARTS, 3)),
            dma,
            dma((3 * PARTS,)),
            dma((3 * PARTS,)),
            dma,
            dma((3,)),
            dma((3,)),
            dma,
        ],
        compiler_params=pltpu.CompilerParams(
            collective_id=0, has_side_effects=True, vmem_limit_bytes=60 * 2**20
        ),
    )(
        adjoint_hat[0],
        velocity.reshape(3, 512, 256),
        vorticity.reshape(3, 512, 256),
        *constants,
    )
    out, grad = pl.pallas_call(
        last_body,
        name="project",
        out_shape=(
            jax.ShapeDtypeStruct((3, 2, KYS, KZS, N), F32),
            jax.ShapeDtypeStruct((3, 6), F32),
        ),
        in_specs=[hbm, pl.BlockSpec(memory_space=pltpu.VMEM)],
        out_specs=(hbm, pl.BlockSpec(memory_space=pltpu.VMEM)),
        scratch_shapes=[
            vmem((KZS, 3, KYS, 512), F32),
            vmem((KZS, 3, 2, KYS, N), F32),
            dma((KZS,)),
            dma,
        ],
        compiler_params=pltpu.CompilerParams(vmem_limit_bytes=60 * 2**20),
    )(spec.reshape(3, KZS, KYS, 512), grad)
    return out.reshape(adjoint_hat.shape), grad


def solution(mesh):
    placed = (
        P("env", None, None, "row", "col", None),
        P("env", None, "row", "col", None),
        P("env", None, "row", "col", None),
    )
    return jax.shard_map(
        shards,
        mesh=mesh,
        in_specs=placed,
        out_specs=(P("env", None, None, "row", "col", None), P()),
        check_vma=False,
    )
```
